256 devices in a mesh: tok: 32 (over z, y_lo, core), tp: 8 (over y_hi, x).
Axes of the slice: x: 4, y: 4 (y_hi: 2, y_lo: 2; y = y_hi * 2 + y_lo), z: 8, core: 2. Of those that a mesh axis runs over, the one named last changes fastest.
Arguments:
- hidden_in: bfloat16 [8192, 4096], P('tok', 'tp'), may hold values from -6 to 6
- norm_gain: float32 [4096], replicated, may hold values from 0.5 to 9, as said below
- w_query: bfloat16 [4096, 4096], P(None, 'tp'), may hold values from -0.09375 to 0.09375
- w_key: bfloat16 [4096, 1024], P(None, 'tp'), may hold values from -0.09375 to 0.09375
- w_value: bfloat16 [4096, 1024], P(None, 'tp'), may hold values from -0.09375 to 0.09375
- w_out: bfloat16 [4096, 4096], P('tp'), may hold values from -0.5 to 0.5
- doc_ids: int32 [8192], replicated, may hold values from 0 to 3, never falling along the last dimension, each value on 1 to 6144 neighbouring positions
Outputs:
- hidden_out: bfloat16 [8192, 4096], P('tok', 'tp')
- joint_cov: float32 [2, 4096, 2, 4096], P(None, 'tok', None, 'tp')
The draws below stay inside these ranges and needn't reach their ends.
Inputs may be any that keep to these rules, and one draw needn't show every extreme that they name: `norm_gain`: each channel's gain is positive. `doc_ids`: document numbers never fall along the tokens; a document holds 1 to 6144 tokens.
All inputs are finite; a program needn't handle non-finite values.
Results may differ from the reference program's by a relative error of at most 0.013.
The reference program's roundings to bfloat16 on the way count: a program that leaves them out, or rounds other values in their place, can miss the bound.
Values may be sent and summed in bfloat16 or wider, within the bound.
No kernel may reach another device: no remote copies, remote signals or barrier semaphores. Data moves between devices by JAX's collectives and lax.ppermute only.
A program may use at most 128 MiB of HBM per device.

```python
import math
import jax
import jax.numpy as jnp
import numpy as np
from jax import lax

D = 4096
HEADS = 32
KV_HEADS = 8
HS = 128
TOKENS = 8192
SEQ = 8192


def draw_norm_gain(key, part):
    return jnp.exp(jax.random.uniform(key, (D,), jnp.float32, jnp.log(0.5), jnp.log(2.0)))


def levels(key, extent, pieces, least, top_value):
    gain, own = 1.0, jax.random.fold_in(key, 6)
    for dim, blocks in pieces:
        heights = jnp.exp(jax.random.uniform(jax.random.fold_in(own, dim), (blocks,), jnp.float32, least / len(pieces), top_value / len(pieces)))
        gain = gain * jnp.repeat(heights, extent[dim] // blocks).reshape([-1 if axis == dim else 1 for axis in range(len(extent))])
    return gain


def length_profile(count, total, limit, lean):
    portions = [(1 << 20) // math.isqrt(grade ** lean) + 1 for grade in range(2, count + 1)]
    spare, given = total - limit - (count - 1), [1] * (count - 1)
    while spare > 0:
        candidates = [i for i in range(count - 1) if given[i] < limit]
        mass, budget = sum([portions[i] for i in candidates]), spare
        for i in candidates:
            addition = min(limit - given[i], max(1, budget * portions[i] // mass), spare)
            given[i] = given[i] + addition
            spare = spare - addition
    return np.array([limit] + given)


def uneven_parts(rng, count, total, bound, skew):
    if count == 2:
        one = jax.random.randint(rng, (), max(1, total - bound), min(bound, total - 1) + 1)
        return jnp.stack([one, total - one])
    lengths = jnp.asarray(length_profile(count, total, bound, skew), jnp.int32)
    pairs = (count - 1) // 2
    source_of, taker = lengths[1:1 + 2 * pairs:2], lengths[2:2 + 2 * pairs:2]
    margin = jnp.minimum(source_of - 1, bound - taker)
    moved = jax.random.randint(jax.random.fold_in(rng, 1), (pairs,), 0, 1 << 20) % (margin + 1)
    lengths = lengths.at[1:1 + 2 * pairs:2].set(source_of - moved).at[2:2 + 2 * pairs:2].set(taker + moved)
    return lengths[jax.random.permutation(jax.random.fold_in(rng, 2), count)]


def scatter_about(rng, extent, width, bound, shards=(), held_as=jnp.bfloat16):
    array = width * jax.random.normal(rng, extent, jnp.float32)
    if shards:
        array = array * levels(rng, extent, shards, -0.22, 0.18)
    return jnp.clip(array, -bound, bound).astype(held_as)


def setup_inputs(seed: int = 0) -> dict:
    key_list = jax.random.split(jax.random.key(seed), 8)
    return {
        "hidden_in": scatter_about(key_list[0], (TOKENS, D), 1.0, 6.0, ((0, 32), (1, 8))),
        "norm_gain": draw_norm_gain(jax.random.fold_in(key_list[7], 71), 0),
        "w_query": scatter_about(key_list[2], (D, HEADS * HS), D ** -0.5, 0.09375, ((1, 8),)),
        "w_key": scatter_about(key_list[3], (D, KV_HEADS * HS), D ** -0.5, 0.09375, ((1, 8),)),
        "w_value": scatter_about(key_list[4], (D, KV_HEADS * HS), D ** -0.5, 0.09375, ((1, 8),)),
        "w_out": scatter_about(key_list[5], (HEADS * HS, D), HS ** -0.5, 0.5, ((0, 8),)),
        "doc_ids": jnp.searchsorted(jnp.cumsum(uneven_parts(key_list[6], 4, TOKENS, 3 * SEQ // 4, 2)), jnp.arange(TOKENS), side="right").astype(jnp.int32),
    }


epsilon = 1e-05
rope_base = 500000.0

def rotate(vectors, positions):
    half_dim = vectors.shape[-1] // 2
    inv_freq = rope_base ** (-(jnp.arange(half_dim, dtype=jnp.float32) * 2.0) / vectors.shape[-1])
    angles = positions.astype(jnp.float32)[:, None] * inv_freq[None, :]
    cosine = jnp.cos(angles)[:, None, :]
    sine_part = jnp.sin(angles)[:, None, :]
    first_half = vectors[..., :half_dim]
    second_half = vectors[..., half_dim:]
    return jnp.concatenate([first_half * cosine - second_half * sine_part, second_half * cosine + first_half * sine_part], axis=-1)

def reference(hidden_in, norm_gain, w_query, w_key, w_value, w_out, doc_ids):
    widened = hidden_in.astype(jnp.float32)
    factor = lax.rsqrt(lax.optimization_barrier(jnp.mean(widened * widened, axis=1, keepdims=True)) + epsilon)
    normed = (widened * factor * norm_gain[None, :]).astype(jnp.bfloat16)
    groups = HEADS // KV_HEADS
    positions = jnp.arange(TOKENS, dtype=jnp.int32)
    queries = rotate(jnp.dot(normed, w_query, preferred_element_type=jnp.float32).reshape(TOKENS, HEADS, HS), positions % SEQ)
    queries = queries.astype(jnp.bfloat16).reshape(TOKENS, KV_HEADS, groups, HS)
    key_rows = rotate(jnp.dot(normed, w_key, preferred_element_type=jnp.float32).reshape(TOKENS, KV_HEADS, HS), positions % SEQ).astype(jnp.bfloat16)
    value_rows = jnp.dot(normed, w_value, preferred_element_type=jnp.float32).astype(jnp.bfloat16).reshape(TOKENS, KV_HEADS, HS)
    block_size = SEQ // 16
    key_wide = key_rows.astype(jnp.float32)
    value_wide = value_rows.astype(jnp.float32)

    def attend(number):
        anchor = (number * block_size).astype(jnp.int32)
        seq_anchor = (anchor // SEQ * SEQ).astype(jnp.int32)
        query_part = lax.dynamic_slice_in_dim(queries, anchor, block_size, 0).astype(jnp.float32)
        query_pos = anchor + jnp.arange(block_size, dtype=jnp.int32)
        query_doc = lax.dynamic_slice_in_dim(doc_ids, anchor, block_size, 0)
        key_pos = seq_anchor + jnp.arange(SEQ, dtype=jnp.int32)
        key_doc = lax.dynamic_slice_in_dim(doc_ids, seq_anchor, SEQ, 0)
        key_part = lax.dynamic_slice_in_dim(key_wide, seq_anchor, SEQ, 0)
        value_part = lax.dynamic_slice_in_dim(value_wide, seq_anchor, SEQ, 0)
        allowed = (query_doc[:, None] == key_doc[None, :]) & (key_pos[None, :] <= query_pos[:, None])
        scores = jnp.einsum('qhgd,khd->hgqk', query_part, key_part) * HS ** (-0.5)
        scores = jnp.where(allowed[None, None], scores, -jnp.inf)
        row_max = lax.optimization_barrier(jnp.max(scores, axis=-1, keepdims=True))
        weights = jnp.exp(scores - row_max)
        weight_sum = lax.optimization_barrier(jnp.sum(weights, axis=-1, keepdims=True))
        rounded = lax.optimization_barrier(weights.astype(jnp.bfloat16)).astype(jnp.float32)
        blended = jnp.einsum('hgqk,khd->hgqd', rounded, value_part) / weight_sum
        return jnp.transpose(blended, (2, 0, 1, 3)).astype(jnp.bfloat16)
    attended = lax.map(attend, jnp.arange(TOKENS // block_size, dtype=jnp.int32)).reshape(TOKENS, HEADS * HS)
    layer_sum = jnp.dot(attended, w_out, preferred_element_type=jnp.float32)
    hidden_out = (widened + layer_sum).astype(jnp.bfloat16)
    joint_rows = jnp.stack([hidden_in, hidden_out], axis=1).reshape(TOKENS, 2 * D)
    gram_block = lax.dot_general(joint_rows, joint_rows, (((0,), (0,)), ((), ())), preferred_element_type=jnp.float32)
    means = lax.optimization_barrier(jnp.sum(joint_rows, axis=0, dtype=jnp.float32)) / TOKENS
    joint_cov = (gram_block / TOKENS - means[:, None] * means[None, :]).reshape(2, D, 2, D)
    return (hidden_out, joint_cov)
```

```python
import functools
import math

import jax
import jax.numpy as jnp
from jax import lax
from jax.experimental import pallas as pl
from jax.experimental.pallas import tpu as pltpu
from jax.sharding import PartitionSpec as P

HS = 128
EPS = 1e-05
ROPE_BASE = 500000.0
NEG = -1e30
F32 = jnp.float32
BF16 = jnp.bfloat16

NZ, NY, NC, NTP = 8, 2, 2, 8
ROWS = 256
COLS = 512
HALF = 256
HEADS = 4
BOTH = ("tok", "tp")
VMEM = pl.BlockSpec(memory_space=pltpu.VMEM)
SMEM = pl.BlockSpec(memory_space=pltpu.SMEM)
ANY = pl.BlockSpec(memory_space=pl.ANY)


def tok_of(z, y, k):
    return (z * NY + y) * NC + k


CELLS = [(z, y, k) for z in range(NZ) for y in range(NY) for k in range(NC)]
UP = [(tok_of(z, y, k), tok_of((z + 1) % NZ, y, k)) for z, y, k in CELLS]
DOWN = [(b, a) for a, b in UP]
OTHER_Y = [(tok_of(z, y, k), tok_of(z, 1 - y, k)) for z, y, k in CELLS]
OTHER_CORE = [(tok_of(z, y, k), tok_of(z, y, 1 - k)) for z, y, k in CELLS]
SAME_CORE = [[tok_of(z, y, k) for z in range(NZ) for y in range(NY)] for k in range(NC)]
TO_PLANE = [
    (tok_of(z, y, k) * NTP + c, tok_of(c, y, k) * NTP + (z ^ c))
    for z, y, k in CELLS
    for c in range(NTP)
]


def params(mib, **kw):
    return pltpu.CompilerParams(vmem_limit_bytes=mib << 20, **kw)


def gather_tp(x):
    copies = jnp.broadcast_to(x, (NTP, *x.shape))
    return lax.all_to_all(copies, "tp", split_axis=0, concat_axis=0, tiled=True)


def ring(x):
    got, up, down = [(0, 0, x)], x, x
    for step in range(1, NZ // 2):
        up, down = lax.ppermute(up, "tok", UP), lax.ppermute(down, "tok", DOWN)
        got += [(step, 0, up), (NZ - step, 0, down)]
    middle = x.shape[0] // 2
    got.append((NZ // 2, 0, lax.ppermute(up[:middle], "tok", UP)))
    got.append((NZ // 2, middle, lax.ppermute(down[middle:], "tok", DOWN)))
    return got


def in_y_order(mine, other, y):
    return jnp.where(y == 0, jnp.concatenate([mine, other]), jnp.concatenate([other, mine]))


def turned(x, cos, sin):
    return x * cos + pltpu.roll(x, HS // 2, 1) * sin


def norm_kv_kernel(x_ref, gain_ref, wk_ref, wv_ref, cos_ref, sin_ref, normed_ref, kv_ref):
    total = jnp.zeros((ROWS, 1), F32)
    for c in range(NTP):
        x = x_ref[c].astype(F32)
        total += jnp.sum(x * x, axis=1, keepdims=True)
    factor = lax.rsqrt(total / (NTP * COLS) + EPS)
    k = jnp.zeros((ROWS, HS), F32)
    v = jnp.zeros((ROWS, HS), F32)
    for c in range(NTP):
        normed = (x_ref[c].astype(F32) * factor * gain_ref[c : c + 1, :]).astype(BF16)
        normed_ref[c] = normed
        k += jnp.dot(normed, wk_ref[c * COLS : (c + 1) * COLS, :], preferred_element_type=F32)
        v += jnp.dot(normed, wv_ref[c * COLS : (c + 1) * COLS, :], preferred_element_type=F32)
    kv_ref[:ROWS, :] = turned(k, cos_ref[...], sin_ref[...]).astype(BF16)
    kv_ref[ROWS:, :] = v.astype(BF16)


def query_kernel(normed_ref, wq_ref, cos_ref, sin_ref, q_ref, acc):
    c = pl.program_id(0)
    part = jnp.dot(normed_ref[0], wq_ref[...], preferred_element_type=F32)

    @pl.when(c == 0)
    def _():
        acc[...] = part

    @pl.when(c > 0)
    def _():
        acc[...] += part

    @pl.when(c == NTP - 1)
    def _():
        for h in range(HEADS):
            q = turned(acc[:, h * HS : (h + 1) * HS], cos_ref[...], sin_ref[...])
            q_ref[:, h * ROWS : (h + 1) * ROWS] = q.T.astype(BF16)


def attend_kernel(places, where_ref, starts_ref, q_mine_ref, q_other_ref, *rest):
    n = len(places)
    kv_refs, (mine_ref, mine_stat, other_ref, other_stat, kv, sems) = rest[:n], rest[n:]
    z, y, k = where_ref[0], where_ref[1], where_ref[2]
    scale = math.log2(math.e) * HS**-0.5
    copies = []
    for i, ((far, row, own), ref) in enumerate(zip(places, kv_refs)):
        at = lax.rem(z + NZ - far, NZ) * NY + (y if own else 1 - y)
        copies.append(
            pltpu.make_async_copy(ref, kv.at[at, pl.ds(row, ref.shape[0])], sems.at[i])
        )
    for copy in copies:
        copy.start()
    for ref in (mine_ref, other_ref):
        ref[...] = jnp.zeros_like(ref)
    for ref in (mine_stat, other_stat):
        ref[0:1, :] = jnp.full((1, HEADS * ROWS), NEG, F32)
        ref[1:2, :] = jnp.zeros((1, HEADS * ROWS), F32)
    for copy in copies:
        copy.wait()

    for tile, (q_ref, acc_ref, stat_ref) in enumerate(
        ((q_mine_ref, mine_ref, mine_stat), (q_other_ref, other_ref, other_stat))
    ):
        core = k if tile == 0 else 1 - k
        q_at = ((z * NY + y) * NC + core) * ROWS
        first, last = where_ref[3 + 2 * tile], where_ref[4 + 2 * tile]
        starts = starts_ref[tile : tile + 1, :]

        def block(b, masked):
            k_at = (b * NC + k) * ROWS
            keys, values = kv[b, :ROWS, :], kv[b, ROWS:, :]
            if masked:
                key_pos = k_at + lax.broadcasted_iota(jnp.int32, (ROWS, ROWS), 0)
                query_pos = q_at + lax.broadcasted_iota(jnp.int32, (ROWS, ROWS), 1)
                kept = (key_pos <= query_pos) & (key_pos >= starts)
            for h in range(HEADS):
                at = slice(h * ROWS, (h + 1) * ROWS)
                s = jnp.dot(keys, q_ref[:, at], preferred_element_type=F32)
                if masked:
                    s = jnp.where(kept, s, NEG)
                old = stat_ref[0:1, at]
                top = jnp.maximum(old, jnp.max(s, axis=0, keepdims=True) * scale)
                w = jnp.exp2(s * scale - top)
                fade = jnp.exp2(old - top)
                stat_ref[0:1, at] = top
                stat_ref[1:2, at] = stat_ref[1:2, at] * fade + jnp.sum(w, axis=0, keepdims=True)
                acc_ref[:, at] = acc_ref[:, at] * fade + lax.dot_general(
                    values, w.astype(BF16), (((0,), (0,)), ((), ())), preferred_element_type=F32
                )

        @pl.loop(0, NZ * NY)
        def _(b):
            k_at = (b * NC + k) * ROWS
            needed = (k_at <= q_at) & (k_at + ROWS > first)
            whole = (k_at < q_at) & (k_at >= last)

            @pl.when(needed & whole)
            def _():
                block(b, False)

            @pl.when(needed & jnp.logical_not(whole))
            def _():
                block(b, True)


def project_kernel(mine_ref, mine_stat, came_ref, came_stat, w_ref, out_ref, att):
    @pl.when(pl.program_id(0) == 0)
    def _():
        for h in range(HEADS):
            at = slice(h * ROWS, (h + 1) * ROWS)
            a, b = mine_stat[0:1, at], came_stat[0:1, at]
            top = jnp.maximum(a, b)
            fa, fb = jnp.exp2(a - top), jnp.exp2(b - top)
            weight_sum = mine_stat[1:2, at] * fa + came_stat[1:2, at] * fb
            blended = (mine_ref[:, at] * fa + came_ref[:, at] * fb) / weight_sum
            att[:, h * HS : (h + 1) * HS] = blended.T.astype(BF16)

    out_ref[0] = jnp.dot(att[...], w_ref[...], preferred_element_type=F32).astype(BF16)


def cross(rows, cols):
    return lax.dot_general(rows, cols, (((0,), (0,)), ((), ())), preferred_element_type=F32)


def split_rows(acc, k, mine_ref, other_ref):
    mine_ref[...] = acc[pl.ds(pl.multiple_of(k * HS, HS), HS), :]
    other_ref[...] = acc[pl.ds(pl.multiple_of((1 - k) * HS, HS), HS), :]


def gram_in_kernel(where_ref, rows_ref, cols_ref, mine_ref, other_ref, acc):
    z, k = where_ref[0], where_ref[2]
    acc[...] = jnp.zeros_like(acc)

    @pl.loop(0, NZ)
    def _(plane):
        acc[...] += cross(rows_ref[jnp.bitwise_xor(plane, z)], cols_ref[plane])

    split_rows(acc, k, mine_ref, other_ref)


def gram_kernel(places, where_ref, rows_in_ref, rows_out_ref, cols_in_ref, *rest):
    n = len(places)
    refs, rest = rest[:n], rest[n:]
    (mine_io, other_io, mine_oi, other_oi, mine_oo, other_oo, row_sum, col_sum) = rest[:8]
    cols, io, oi, oo, sems = rest[8:]
    z, y, k = where_ref[0], where_ref[1], where_ref[2]
    copies = []
    for i, ((far, row, own), ref) in enumerate(zip(places, refs)):
        at = lax.rem(z + NZ - far, NZ)
        start = pl.multiple_of((y if own else 1 - y) * ROWS + row, HS)
        copies.append(
            pltpu.make_async_copy(ref, cols.at[at, pl.ds(start, ref.shape[0])], sems.at[i])
        )
    for copy in copies:
        copy.start()
    for ref in (io, oi, oo, row_sum, col_sum):
        ref[...] = jnp.zeros_like(ref)
    for copy in copies:
        copy.wait()

    @pl.loop(0, NZ)
    def _(plane):
        here = jnp.bitwise_xor(plane, z)
        rows_in, rows_out = rows_in_ref[here], rows_out_ref[here]
        cols_in, cols_out = cols_in_ref[plane], cols[plane]
        io[...] += cross(rows_in, cols_out)
        oi[...] += cross(rows_out, cols_in)
        oo[...] += cross(rows_out, cols_out)
        for x, ref, at in (
            (rows_in, row_sum, slice(0, HALF)),
            (rows_out, row_sum, slice(HALF, 2 * HALF)),
            (cols_in, col_sum, slice(0, COLS)),
            (cols_out, col_sum, slice(COLS, 2 * COLS)),
        ):
            ref[0:1, at] += jnp.sum(x.astype(F32), axis=0, keepdims=True)

    split_rows(io, k, mine_io, other_io)
    split_rows(oi, k, mine_oi, other_oi)
    split_rows(oo, k, mine_oo, other_oo)


def on_device(hidden_in, norm_gain, w_query, w_key, w_value, w_out, doc_ids):
    tok_index = lax.axis_index("tok")
    z, y, k = tok_index // (NY * NC), (tok_index // NC) % NY, tok_index % NC
    tokens = ROWS * NZ * NY * NC

    first_row = tok_index * ROWS
    other_row = (tok_index + 1 - 2 * k) * ROWS
    doc_start = jnp.stack([jnp.sum((doc_ids < d).astype(jnp.int32)) for d in range(4)])

    def starts_of(row):
        docs = lax.dynamic_slice_in_dim(doc_ids, row, ROWS, 0)
        return sum(jnp.where(docs == d, doc_start[d], 0) for d in range(4))

    starts = jnp.stack([starts_of(first_row), starts_of(other_row)])
    place = jnp.stack([z, y, k]).astype(jnp.int32)
    ends = jnp.stack([starts[0, 0], starts[0, -1], starts[1, 0], starts[1, -1]])
    where = jnp.concatenate([place, ends]).astype(jnp.int32)
    inv_freq = ROPE_BASE ** (-(jnp.arange(HS // 2, dtype=F32) * 2.0) / HS)
    positions = first_row + jnp.arange(ROWS, dtype=jnp.int32)
    angles = positions.astype(F32)[:, None] * inv_freq[None, :]
    cosine, sine = jnp.cos(angles), jnp.sin(angles)
    cos = jnp.concatenate([cosine, cosine], axis=1)
    sin = jnp.concatenate([-sine, sine], axis=1)

    full_in = gather_tp(hidden_in)
    normed, kv = pl.pallas_call(
        norm_kv_kernel,
        out_shape=(
            jax.ShapeDtypeStruct((NTP, ROWS, COLS), BF16),
            jax.ShapeDtypeStruct((2 * ROWS, HS), BF16),
        ),
        in_specs=[VMEM] * 6,
        out_specs=(VMEM, VMEM),
        compiler_params=params(32),
        name="norm_kv",
    )(full_in, norm_gain.reshape(NTP, COLS), w_key, w_value, cos, sin)
    kv_other = lax.ppermute(kv, "tok", OTHER_Y)
    kv_blocks = [(f, r, True, b) for f, r, b in ring(kv)]
    kv_blocks += [(f, r, False, b) for f, r, b in ring(kv_other)]

    q = pl.pallas_call(
        query_kernel,
        grid=(NTP,),
        out_shape=jax.ShapeDtypeStruct((HS, HEADS * ROWS), BF16),
        in_specs=[
            pl.BlockSpec((1, ROWS, COLS), lambda c: (c, 0, 0)),
            pl.BlockSpec((COLS, HEADS * HS), lambda c: (c, 0)),
            pl.BlockSpec((ROWS, HS), lambda c: (0, 0)),
            pl.BlockSpec((ROWS, HS), lambda c: (0, 0)),
        ],
        out_specs=pl.BlockSpec((HS, HEADS * ROWS), lambda c: (0, 0)),
        scratch_shapes=[pltpu.VMEM((ROWS, HEADS * HS), F32)],
        compiler_params=params(32),
        name="queries",
    )(normed, w_query, cos, sin)
    q_other = lax.ppermute(q, "tok", OTHER_CORE)

    def rows_of(x):
        mine = lax.dynamic_slice_in_dim(x, y * HALF, HALF, 1)
        theirs = lax.dynamic_slice_in_dim(x, (1 - y) * HALF, HALF, 1)
        both = in_y_order(mine, lax.ppermute(theirs, "tok", OTHER_Y), y)
        return gather_tp(lax.ppermute(both, BOTH, TO_PLANE))

    cols_in = lax.all_gather(
        hidden_in, "tok", axis=0, tiled=True, axis_index_groups=SAME_CORE
    ).reshape(NZ, NY * ROWS, COLS)
    rows_in = rows_of(hidden_in)
    part = jax.ShapeDtypeStruct((HS, COLS), F32)
    acc = pltpu.VMEM((HALF, COLS), F32)
    mine_ii, other_ii = pl.pallas_call(
        gram_in_kernel,
        out_shape=(part, part),
        in_specs=[SMEM, VMEM, VMEM],
        out_specs=(VMEM, VMEM),
        scratch_shapes=[acc],
        compiler_params=params(32),
        name="gram_in",
    )(where, rows_in, cols_in)

    half = jax.ShapeDtypeStruct((HS, HEADS * ROWS), F32)
    stat = jax.ShapeDtypeStruct((8, HEADS * ROWS), F32)
    mine, mine_stat, other, other_stat = pl.pallas_call(
        functools.partial(attend_kernel, [b[:3] for b in kv_blocks]),
        out_shape=(half, stat, half, stat),
        in_specs=[SMEM, VMEM, VMEM, VMEM] + [ANY] * len(kv_blocks),
        out_specs=(VMEM,) * 4,
        scratch_shapes=[
            pltpu.VMEM((NZ * NY, 2 * ROWS, HS), BF16),
            pltpu.SemaphoreType.DMA((len(kv_blocks),)),
        ],
        compiler_params=params(40),
        name="attend",
    )(where, starts, q, q_other, *[b[3] for b in kv_blocks])
    came = lax.ppermute(other, "tok", OTHER_CORE)
    came_stat = lax.ppermute(other_stat, "tok", OTHER_CORE)

    fixed = lambda c: (0, 0)
    partial_out = pl.pallas_call(
        project_kernel,
        grid=(NTP,),
        out_shape=jax.ShapeDtypeStruct((NTP, ROWS, COLS), BF16),
        in_specs=[
            pl.BlockSpec((HS, HEADS * ROWS), fixed),
            pl.BlockSpec((8, HEADS * ROWS), fixed),
            pl.BlockSpec((HS, HEADS * ROWS), fixed),
            pl.BlockSpec((8, HEADS * ROWS), fixed),
            pl.BlockSpec((HEADS * HS, COLS), lambda c: (0, c)),
        ],
        out_specs=pl.BlockSpec((1, ROWS, COLS), lambda c: (c, 0, 0)),
        scratch_shapes=[pltpu.VMEM((ROWS, HEADS * HS), BF16)],
        compiler_params=params(32),
        name="project",
    )(mine, mine_stat, came, came_stat, w_out)
    shares = lax.all_to_all(partial_out, "tp", split_axis=0, concat_axis=0, tiled=True)
    hidden_out = (
        hidden_in.astype(F32) + jnp.sum(shares.astype(F32), axis=0)
    ).astype(BF16)

    out_other = lax.ppermute(hidden_out, "tok", OTHER_Y)
    out_blocks = [(f, r, True, b) for f, r, b in ring(hidden_out)]
    out_blocks += [(f, r, False, b) for f, r, b in ring(out_other)]
    rows_out = rows_of(hidden_out)
    got = pl.pallas_call(
        functools.partial(gram_kernel, [b[:3] for b in out_blocks]),
        out_shape=(part,) * 6
        + (
            jax.ShapeDtypeStruct((8, 2 * HALF), F32),
            jax.ShapeDtypeStruct((8, 2 * COLS), F32),
        ),
        in_specs=[SMEM, VMEM, VMEM, VMEM] + [ANY] * len(out_blocks),
        out_specs=(VMEM,) * 8,
        scratch_shapes=[
            pltpu.VMEM((NZ, NY * ROWS, COLS), BF16),
            acc,
            acc,
            acc,
            pltpu.SemaphoreType.DMA((len(out_blocks),)),
        ],
        compiler_params=params(48),
        name="gram",
    )(where, rows_in, rows_out, cols_in, *[b[3] for b in out_blocks])
    mine_io, other_io, mine_oi, other_oi, mine_oo, other_oo, row_sum, col_sum = got
    swap = lambda x: lax.ppermute(x, "tok", OTHER_CORE)
    total = lambda a, b: (a + swap(b)) / tokens
    row_sum = row_sum[0].reshape(2, NC, HS)
    sums = jnp.concatenate([row_sum.reshape(-1), col_sum[0]]).reshape(12, HS)
    sums = (sums + swap(sums)).reshape(-1) / tokens
    row_mean = lax.dynamic_slice_in_dim(sums[: 2 * HALF].reshape(2, NC, HS), k, 1, 1)[:, 0]
    col_mean = sums[2 * HALF :].reshape(2, COLS)
    gram = jnp.stack(
        [
            jnp.stack([total(mine_ii, other_ii), total(mine_io, other_io)], axis=1),
            jnp.stack([total(mine_oi, other_oi), total(mine_oo, other_oo)], axis=1),
        ]
    )
    joint_cov = gram - row_mean[:, :, None, None] * col_mean[None, None]
    return hidden_out, joint_cov


def solution(mesh):
    return jax.shard_map(
        on_device,
        mesh=mesh,
        in_specs=(
            P("tok", "tp"),
            P(),
            P(None, "tp"),
            P(None, "tp"),
            P(None, "tp"),
            P("tp", None),
            P(),
        ),
        out_specs=(P("tok", "tp"), P(None, "tok", None, "tp")),
        check_vma=False,
    )
```

```python
import functools
import math

import jax
import jax.numpy as jnp
from jax import lax
from jax.experimental import pallas as pl
from jax.experimental.pallas import tpu as pltpu
from jax.sharding import PartitionSpec as P

HS = 128
EPS = 1e-05
ROPE_BASE = 500000.0
NEG = -1e30
F32 = jnp.float32
BF16 = jnp.bfloat16

NZ, NY, NC, NTP = 8, 2, 2, 8
ROWS = 256
COLS = 512
HALF = 256
HEADS = 4
BOTH = ("tok", "tp")
VMEM = pl.BlockSpec(memory_space=pltpu.VMEM)
SMEM = pl.BlockSpec(memory_space=pltpu.SMEM)
ANY = pl.BlockSpec(memory_space=pl.ANY)


def tok_of(z, y, k):
    return (z * NY + y) * NC + k


CELLS = [(z, y, k) for z in range(NZ) for y in range(NY) for k in range(NC)]
UP = [(tok_of(z, y, k), tok_of((z + 1) % NZ, y, k)) for z, y, k in CELLS]
DOWN = [(b, a) for a, b in UP]
OTHER_Y = [(tok_of(z, y, k), tok_of(z, 1 - y, k)) for z, y, k in CELLS]
OTHER_CORE = [(tok_of(z, y, k), tok_of(z, y, 1 - k)) for z, y, k in CELLS]
ALONG_Z = [[tok_of(z, y, k) for z in range(NZ)] for y in range(NY) for k in range(NC)]
TO_PLANE = [
    (tok_of(z, y, k) * NTP + c, tok_of(c, y, k) * NTP + (z + c) % NTP)
    for z, y, k in CELLS
    for c in range(NTP)
]


def params(mib, **kw):
    return pltpu.CompilerParams(vmem_limit_bytes=mib << 20, **kw)


def cost(flops, moved):
    return pl.CostEstimate(flops=flops, bytes_accessed=moved, transcendentals=0)


def after(x, *earlier):
    return lax.optimization_barrier((x, *earlier))[0]


def gather_tp(x):
    copies = jnp.broadcast_to(x, (NTP, *x.shape))
    return lax.all_to_all(copies, "tp", split_axis=0, concat_axis=0, tiled=True)


def ring(x, meanwhile=None):
    got, up, down = [(0, 0, x)], x, x
    for step in range(1, NZ // 2):
        if step == NZ // 2 - 1 and meanwhile is not None:
            up, down = after(up, meanwhile), after(down, meanwhile)
        up, down = lax.ppermute(up, "tok", UP), lax.ppermute(down, "tok", DOWN)
        got += [(step, 0, up), (NZ - step, 0, down)]
    middle = x.shape[0] // 2
    got.append((NZ // 2, 0, lax.ppermute(up[:middle], "tok", UP)))
    got.append((NZ // 2, middle, lax.ppermute(down[middle:], "tok", DOWN)))
    return got


def turned(x, cos, sin):
    return x * cos + pltpu.roll(x, HS // 2, 1) * sin


def norm_kv_kernel(x_ref, gain_ref, wk_ref, wv_ref, cos_ref, sin_ref, normed_ref, kv_ref):
    total = jnp.zeros((ROWS, 1), F32)
    for c in range(NTP):
        x = x_ref[c].astype(F32)
        total += jnp.sum(x * x, axis=1, keepdims=True)
    factor = lax.rsqrt(total / (NTP * COLS) + EPS)
    k = jnp.zeros((ROWS, HS), F32)
    v = jnp.zeros((ROWS, HS), F32)
    for c in range(NTP):
        normed = (x_ref[c].astype(F32) * factor * gain_ref[c : c + 1, :]).astype(BF16)
        normed_ref[c] = normed
        k += jnp.dot(normed, wk_ref[c * COLS : (c + 1) * COLS, :], preferred_element_type=F32)
        v += jnp.dot(normed, wv_ref[c * COLS : (c + 1) * COLS, :], preferred_element_type=F32)
    kv_ref[:ROWS, :] = turned(k, cos_ref[...], sin_ref[...]).astype(BF16)
    kv_ref[ROWS:, :] = v.astype(BF16)


def query_kernel(normed_ref, wq_ref, cos_ref, sin_ref, q_ref, acc):
    c = pl.program_id(0)
    part = jnp.dot(normed_ref[0], wq_ref[...], preferred_element_type=F32)

    @pl.when(c == 0)
    def _():
        acc[...] = part

    @pl.when(c > 0)
    def _():
        acc[...] += part

    @pl.when(c == NTP - 1)
    def _():
        for h in range(HEADS):
            q = turned(acc[:, h * HS : (h + 1) * HS], cos_ref[...], sin_ref[...])
            q_ref[:, h * ROWS : (h + 1) * ROWS] = q.T.astype(BF16)


def land(places, z, refs, held, sems):
    copies = []
    for i, ((far, row), ref) in enumerate(zip(places, refs)):
        at = lax.rem(z + NZ - far, NZ)
        copies.append(
            pltpu.make_async_copy(ref, held.at[at, pl.ds(row, ref.shape[0])], sems.at[i])
        )
    return copies


def attend_kernel(places, where_ref, starts_ref, q_mine_ref, q_other_ref, *rest):
    n = len(places)
    kv_refs, (mine_ref, other_ref, kv, sems) = rest[:n], rest[n:]
    z, y, k = where_ref[0], where_ref[1], where_ref[2]
    scale = math.log2(math.e) * HS**-0.5
    copies = land(places, z, kv_refs, kv, sems)
    for copy in copies:
        copy.start()
    for ref in (mine_ref, other_ref):
        ref[...] = jnp.zeros_like(ref)
        ref[HS : HS + 1, :] = jnp.full((1, HEADS * ROWS), NEG, F32)
    for copy in copies:
        copy.wait()

    for tile, (q_ref, acc_ref) in enumerate(((q_mine_ref, mine_ref), (q_other_ref, other_ref))):
        core = k if tile == 0 else 1 - k
        q_at = ((z * NY + y) * NC + core) * ROWS
        first, last = where_ref[3 + 2 * tile], where_ref[4 + 2 * tile]
        starts = starts_ref[tile : tile + 1, :]

        def block(plane, j, masked):
            k_at = ((plane * NY + lax.rem(y + j, NY)) * NC + k) * ROWS
            keys = kv[plane, 2 * j * ROWS : (2 * j + 1) * ROWS, :]
            values = kv[plane, (2 * j + 1) * ROWS : (2 * j + 2) * ROWS, :]
            if masked:
                key_pos = k_at + lax.broadcasted_iota(jnp.int32, (ROWS, ROWS), 0)
                query_pos = q_at + lax.broadcasted_iota(jnp.int32, (ROWS, ROWS), 1)
                kept = (key_pos <= query_pos) & (key_pos >= starts)
            for h in range(HEADS):
                at = slice(h * ROWS, (h + 1) * ROWS)
                s = jnp.dot(keys, q_ref[:, at], preferred_element_type=F32)
                if masked:
                    s = jnp.where(kept, s, NEG)
                old = acc_ref[HS : HS + 1, at]
                top = jnp.maximum(old, jnp.max(s, axis=0, keepdims=True) * scale)
                w = jnp.exp2(s * scale - top)
                fade = jnp.exp2(old - top)
                acc_ref[HS : HS + 1, at] = top
                acc_ref[HS + 1 : HS + 2, at] = acc_ref[HS + 1 : HS + 2, at] * fade + jnp.sum(
                    w, axis=0, keepdims=True
                )
                acc_ref[:HS, at] = acc_ref[:HS, at] * fade + lax.dot_general(
                    values, w.astype(BF16), (((0,), (0,)), ((), ())), preferred_element_type=F32
                )

        @pl.loop(0, NZ)
        def _(plane):
            for j in range(NY):
                k_at = ((plane * NY + lax.rem(y + j, NY)) * NC + k) * ROWS
                needed = (k_at <= q_at) & (k_at + ROWS > first)
                whole = (k_at < q_at) & (k_at >= last)

                @pl.when(needed & whole)
                def _():
                    block(plane, j, False)

                @pl.when(needed & jnp.logical_not(whole))
                def _():
                    block(plane, j, True)


def project_kernel(mine_ref, came_ref, w_ref, out_ref, att):
    @pl.when(pl.program_id(0) == 0)
    def _():
        for h in range(HEADS):
            at = slice(h * ROWS, (h + 1) * ROWS)
            a, b = mine_ref[HS : HS + 1, at], came_ref[HS : HS + 1, at]
            top = jnp.maximum(a, b)
            fa, fb = jnp.exp2(a - top), jnp.exp2(b - top)
            weight_sum = mine_ref[HS + 1 : HS + 2, at] * fa + came_ref[HS + 1 : HS + 2, at] * fb
            blended = (mine_ref[:HS, at] * fa + came_ref[:HS, at] * fb) / weight_sum
            att[:, h * HS : (h + 1) * HS] = blended.T.astype(BF16)

    out_ref[0] = jnp.dot(att[...], w_ref[...], preferred_element_type=F32).astype(BF16)


def cross(rows, cols):
    return lax.dot_general(rows, cols, (((0,), (0,)), ((), ())), preferred_element_type=F32)


def sum_of(x):
    return jnp.sum(x.astype(F32), axis=0, keepdims=True)


def gram_in_kernel(where_ref, rows_ref, cols_ref, acc, sums):
    z = where_ref[0]
    acc[...] = jnp.zeros_like(acc)
    sums[...] = jnp.zeros_like(sums)

    @pl.loop(0, NZ)
    def _(plane):
        rows, cols = rows_ref[lax.rem(plane + z, NTP)], cols_ref[plane]
        acc[...] += cross(rows, cols)
        sums[0:1, :HALF] += sum_of(rows)
        sums[1:2, :] += sum_of(cols)


def gram_kernel(places, where_ref, rows_in_ref, rows_out_ref, cols_in_ref, ii, sums_in, *rest):
    n = len(places)
    refs, (mine_ref, other_ref, cols, io, oi, oo, sums, sems) = rest[:n], rest[n:]
    z, k = where_ref[0], where_ref[2]
    copies = land(places, z, refs, cols, sems)
    for copy in copies:
        copy.start()
    for ref in (io, oi, oo, sums):
        ref[...] = jnp.zeros_like(ref)
    for copy in copies:
        copy.wait()

    @pl.loop(0, NZ)
    def _(plane):
        here = lax.rem(plane + z, NTP)
        rows_out, cols_out = rows_out_ref[here], cols[plane]
        io[...] += cross(rows_in_ref[here], cols_out)
        oi[...] += cross(rows_out, cols_in_ref[plane])
        oo[...] += cross(rows_out, cols_out)
        sums[0:1, :HALF] += sum_of(rows_out)
        sums[1:2, :] += sum_of(cols_out)

    for core, ref in ((k, mine_ref), (1 - k, other_ref)):
        rows = pl.ds(pl.multiple_of(core * HS, HS), HS)
        ref[:HS, :COLS] = ii[rows, :]
        ref[:HS, COLS:] = io[rows, :]
        ref[HS : 2 * HS, :COLS] = oi[rows, :]
        ref[HS : 2 * HS, COLS:] = oo[rows, :]
        ref[2 * HS :, :] = jnp.zeros((8, 2 * COLS), F32)
        ref[2 * HS : 2 * HS + 1, :COLS] = sums_in[1:2, :]
        ref[2 * HS : 2 * HS + 1, COLS:] = sums[1:2, :]
        for at, x in ((0, sums_in), (HS, sums)):
            ref[2 * HS + 1 : 2 * HS + 2, at : at + HS] = jnp.where(
                core == 0, x[0:1, :HS], x[0:1, HS:HALF]
            )


def finish_kernel(tokens, mine_ref, came_ref, out_ref):
    sums = (mine_ref[2 * HS :, :] + came_ref[2 * HS :, :]) / tokens
    row_mean = sums[:, : 2 * HS].T[:, 1:2]
    for a in range(2):
        for b in range(2):
            rows, cols = slice(a * HS, (a + 1) * HS), slice(b * COLS, (b + 1) * COLS)
            gram = mine_ref[rows, cols] + came_ref[rows, cols]
            out_ref[a, :, b, :] = gram / tokens - row_mean[rows, :] * sums[0:1, cols]


def on_device(hidden_in, norm_gain, w_query, w_key, w_value, w_out, doc_ids):
    tok_index = lax.axis_index("tok")
    z, y, k = tok_index // (NY * NC), (tok_index // NC) % NY, tok_index % NC
    tokens = ROWS * NZ * NY * NC

    first_row = tok_index * ROWS
    other_row = (tok_index + 1 - 2 * k) * ROWS
    doc_start = jnp.stack([jnp.sum((doc_ids < d).astype(jnp.int32)) for d in range(4)])

    def starts_of(row):
        docs = lax.dynamic_slice_in_dim(doc_ids, row, ROWS, 0)
        return sum(jnp.where(docs == d, doc_start[d], 0) for d in range(4))

    starts = jnp.stack([starts_of(first_row), starts_of(other_row)])
    place = jnp.stack([z, y, k]).astype(jnp.int32)
    ends = jnp.stack([starts[0, 0], starts[0, -1], starts[1, 0], starts[1, -1]])
    where = jnp.concatenate([place, ends]).astype(jnp.int32)
    inv_freq = ROPE_BASE ** (-(jnp.arange(HS // 2, dtype=F32) * 2.0) / HS)
    positions = first_row + jnp.arange(ROWS, dtype=jnp.int32)
    angles = positions.astype(F32)[:, None] * inv_freq[None, :]
    cosine, sine = jnp.cos(angles), jnp.sin(angles)
    cos = jnp.concatenate([cosine, cosine], axis=1)
    sin = jnp.concatenate([-sine, sine], axis=1)

    full_in = gather_tp(hidden_in)
    in_pair = jnp.concatenate([hidden_in, lax.ppermute(hidden_in, "tok", OTHER_Y)])
    cols_in = lax.all_gather(in_pair, "tok", axis=0, tiled=True, axis_index_groups=ALONG_Z)
    cols_in = cols_in.reshape(NZ, NY * ROWS, COLS)
    full_in = after(full_in, cos, sin, where, starts, in_pair)
    normed, kv = pl.pallas_call(
        norm_kv_kernel,
        out_shape=(
            jax.ShapeDtypeStruct((NTP, ROWS, COLS), BF16),
            jax.ShapeDtypeStruct((2 * ROWS, HS), BF16),
        ),
        in_specs=[VMEM] * 6,
        out_specs=(VMEM, VMEM),
        compiler_params=params(32),
        cost_estimate=cost(1 << 30, 6 << 20),
        name="norm_kv",
    )(full_in, norm_gain.reshape(NTP, COLS), w_key, w_value, cos, sin)
    kv_pair = jnp.concatenate([kv, lax.ppermute(kv, "tok", OTHER_Y)])

    q = pl.pallas_call(
        query_kernel,
        grid=(NTP,),
        out_shape=jax.ShapeDtypeStruct((HS, HEADS * ROWS), BF16),
        in_specs=[
            pl.BlockSpec((1, ROWS, COLS), lambda c: (c, 0, 0)),
            pl.BlockSpec((COLS, HEADS * HS), lambda c: (c, 0)),
            pl.BlockSpec((ROWS, HS), lambda c: (0, 0)),
            pl.BlockSpec((ROWS, HS), lambda c: (0, 0)),
        ],
        out_specs=pl.BlockSpec((HS, HEADS * ROWS), lambda c: (0, 0)),
        scratch_shapes=[pltpu.VMEM((ROWS, HEADS * HS), F32)],
        compiler_params=params(32),
        cost_estimate=cost(1 << 30, 6 << 20),
        name="queries",
    )(normed, w_query, cos, sin)
    kv_blocks = ring(kv_pair, q)

    def rows_to_plane(pair):
        return lax.ppermute(lax.dynamic_slice_in_dim(pair, y * HALF, HALF, 1), BOTH, TO_PLANE)

    rows_in = after(rows_to_plane(after(in_pair, kv_pair)), kv_blocks[-1][2], kv_blocks[-2][2], cols_in)
    q_other = lax.ppermute(q, "tok", OTHER_CORE)

    half = jax.ShapeDtypeStruct((HS + 8, HEADS * ROWS), F32)
    mine, other = pl.pallas_call(
        functools.partial(attend_kernel, [b[:2] for b in kv_blocks]),
        out_shape=(half, half),
        in_specs=[SMEM, VMEM, VMEM, VMEM] + [ANY] * len(kv_blocks),
        out_specs=(VMEM, VMEM),
        scratch_shapes=[
            pltpu.VMEM((NZ, 2 * NY * ROWS, HS), BF16),
            pltpu.SemaphoreType.DMA((len(kv_blocks),)),
        ],
        compiler_params=params(40),
        cost_estimate=cost(16 << 30, 6 << 20),
        name="attend",
    )(after(where, rows_in), starts, q, q_other, *[b[2] for b in kv_blocks])
    rows_in = gather_tp(rows_in)
    came = after(lax.ppermute(other, "tok", OTHER_CORE), rows_in)

    fixed = lambda c: (0, 0)
    partial_out = pl.pallas_call(
        project_kernel,
        grid=(NTP,),
        out_shape=jax.ShapeDtypeStruct((NTP, ROWS, COLS), BF16),
        in_specs=[
            pl.BlockSpec((HS + 8, HEADS * ROWS), fixed),
            pl.BlockSpec((HS + 8, HEADS * ROWS), fixed),
            pl.BlockSpec((HEADS * HS, COLS), lambda c: (0, c)),
        ],
        out_specs=pl.BlockSpec((1, ROWS, COLS), lambda c: (c, 0, 0)),
        scratch_shapes=[pltpu.VMEM((ROWS, HEADS * HS), BF16)],
        compiler_params=params(32),
        cost_estimate=cost(1 << 30, 8 << 20),
        name="project",
    )(mine, came, w_out)
    shares = lax.all_to_all(partial_out, "tp", split_axis=0, concat_axis=0, tiled=True)
    hidden_out = (
        hidden_in.astype(F32) + jnp.sum(shares.astype(F32), axis=0)
    ).astype(BF16)

    out_pair = jnp.concatenate([hidden_out, lax.ppermute(hidden_out, "tok", OTHER_Y)])
    rows_out = gather_tp(rows_to_plane(out_pair))
    out_blocks = ring(out_pair)
    part = jax.ShapeDtypeStruct((HALF, COLS), F32)
    sums = jax.ShapeDtypeStruct((8, COLS), F32)
    ii, sums_in = pl.pallas_call(
        gram_in_kernel,
        out_shape=(part, sums),
        in_specs=[SMEM, VMEM, VMEM],
        out_specs=(VMEM, VMEM),
        compiler_params=params(32),
        cost_estimate=cost(1 << 30, 6 << 20),
        name="gram_in",
    )(after(where, out_pair), rows_in, cols_in)
    acc = pltpu.VMEM((HALF, COLS), F32)
    half = jax.ShapeDtypeStruct((2 * HS + 8, 2 * COLS), F32)
    mine, other = pl.pallas_call(
        functools.partial(gram_kernel, [b[:2] for b in out_blocks]),
        out_shape=(half, half),
        in_specs=[SMEM] + [VMEM] * 5 + [ANY] * len(out_blocks),
        out_specs=(VMEM, VMEM),
        scratch_shapes=[
            pltpu.VMEM((NZ, NY * ROWS, COLS), BF16),
            acc,
            acc,
            acc,
            pltpu.VMEM((8, COLS), F32),
            pltpu.SemaphoreType.DMA((len(out_blocks),)),
        ],
        compiler_params=params(48),
        cost_estimate=cost(6 << 30, 14 << 20),
        name="gram",
    )(where, rows_in, rows_out, cols_in, ii, sums_in, *[b[2] for b in out_blocks])
    joint_cov = pl.pallas_call(
        functools.partial(finish_kernel, tokens),
        out_shape=jax.ShapeDtypeStruct((2, HS, 2, COLS), F32),
        in_specs=[VMEM, VMEM],
        out_specs=VMEM,
        compiler_params=params(32),
        cost_estimate=cost(1 << 22, 3 << 20),
        name="finish",
    )(mine, lax.ppermute(other, "tok", OTHER_CORE))
    return hidden_out, joint_cov


def solution(mesh):
    return jax.shard_map(
        on_device,
        mesh=mesh,
        in_specs=(
            P("tok", "tp"),
            P(),
            P(None, "tp"),
            P(None, "tp"),
            P(None, "tp"),
            P("tp", None),
            P(),
        ),
        out_specs=(P("tok", "tp"), P(None, "tok", None, "tp")),
        check_vma=False,
    )
```

```python
import functools
import math

import jax
import jax.numpy as jnp
from jax import lax
from jax.experimental import pallas as pl
from jax.experimental.pallas import tpu as pltpu
from jax.sharding import PartitionSpec as P

HS = 128
EPS = 1e-05
ROPE_BASE = 500000.0
NEG = -1e30
F32 = jnp.float32
BF16 = jnp.bfloat16

NZ, NY, NC, NTP = 8, 2, 2, 8
ROWS = 256
COLS = 512
HALF = 256
HEADS = 4
BOTH = ("tok", "tp")
VMEM = pl.BlockSpec(memory_space=pltpu.VMEM)
SMEM = pl.BlockSpec(memory_space=pltpu.SMEM)
ANY = pl.BlockSpec(memory_space=pl.ANY)


def tok_of(z, y, k):
    return (z * NY + y) * NC + k


CELLS = [(z, y, k) for z in range(NZ) for y in range(NY) for k in range(NC)]
UP = [(tok_of(z, y, k), tok_of((z + 1) % NZ, y, k)) for z, y, k in CELLS]
DOWN = [(b, a) for a, b in UP]
OTHER_Y = [(tok_of(z, y, k), tok_of(z, 1 - y, k)) for z, y, k in CELLS]
OTHER_CORE = [(tok_of(z, y, k), tok_of(z, y, 1 - k)) for z, y, k in CELLS]
IN_PLANE = [
    (tok_of(z, y, k) * NTP + c, tok_of(z, y, k) * NTP + (z + c) % NTP)
    for z, y, k in CELLS
    for c in range(NTP)
]
IN_PLANE_OTHER_Y = [
    (tok_of(z, y, k) * NTP + c, tok_of(z, 1 - y, k) * NTP + (z + c) % NTP)
    for z, y, k in CELLS
    for c in range(NTP)
]
TO_PLANE = [
    (tok_of(z, y, k) * NTP + (z + c) % NTP, tok_of(c, y, k) * NTP + (z + c) % NTP)
    for z, y, k in CELLS
    for c in range(NTP)
]


def params(mib, **kw):
    return pltpu.CompilerParams(vmem_limit_bytes=mib << 20, **kw)


def cost(flops, moved):
    return pl.CostEstimate(flops=flops, bytes_accessed=moved, transcendentals=0)


def after(x, *earlier):
    return lax.optimization_barrier((x, *earlier))[0]


def copies_for_tp(x):
    return jnp.broadcast_to(x, (NTP, *x.shape))


def gather_tp(copies):
    return lax.all_to_all(copies, "tp", split_axis=0, concat_axis=0, tiled=True)


def ring(x, meanwhile=()):
    got, up, down = [(0, 0, x)], x, x
    for step in range(1, NZ // 2):
        if step in meanwhile:
            up, down = after(up, *meanwhile[step]), after(down, *meanwhile[step])
        up, down = lax.ppermute(up, "tok", UP), lax.ppermute(down, "tok", DOWN)
        got += [(step, 0, up), (NZ - step, 0, down)]
    middle = x.shape[0] // 2
    got.append((NZ // 2, 0, lax.ppermute(up[:middle], "tok", UP)))
    got.append((NZ // 2, middle, lax.ppermute(down[middle:], "tok", DOWN)))
    return got


def turned(x, cos, sin):
    return x * cos + pltpu.roll(x, HS // 2, 1) * sin


def norm_kv_kernel(x_ref, gain_ref, wk_ref, wv_ref, cos_ref, sin_ref, normed_ref, kv_ref):
    total = jnp.zeros((ROWS, 1), F32)
    for c in range(NTP):
        x = x_ref[c].astype(F32)
        total += jnp.sum(x * x, axis=1, keepdims=True)
    factor = lax.rsqrt(total / (NTP * COLS) + EPS)
    k = jnp.zeros((ROWS, HS), F32)
    v = jnp.zeros((ROWS, HS), F32)
    for c in range(NTP):
        normed = (x_ref[c].astype(F32) * factor * gain_ref[c : c + 1, :]).astype(BF16)
        normed_ref[c] = normed
        k += jnp.dot(normed, wk_ref[c * COLS : (c + 1) * COLS, :], preferred_element_type=F32)
        v += jnp.dot(normed, wv_ref[c * COLS : (c + 1) * COLS, :], preferred_element_type=F32)
    kv_ref[:ROWS, :] = turned(k, cos_ref[...], sin_ref[...]).astype(BF16)
    kv_ref[ROWS:, :] = v.astype(BF16)


def query_kernel(normed_ref, wq_ref, cos_ref, sin_ref, q_ref, weights, sems):
    def copy(c):
        part = pl.ds(c * COLS, COLS)
        return pltpu.make_async_copy(wq_ref.at[part], weights.at[part], sems.at[c])

    for c in range(NTP):
        copy(c).start()
    acc = jnp.zeros((ROWS, HEADS * HS), F32)
    for c in range(NTP):
        copy(c).wait()
        part = weights[c * COLS : (c + 1) * COLS, :]
        acc += jnp.dot(normed_ref[c], part, preferred_element_type=F32)
    for h in range(HEADS):
        q = turned(acc[:, h * HS : (h + 1) * HS], cos_ref[...], sin_ref[...])
        q_ref[:, h * ROWS : (h + 1) * ROWS] = q.T.astype(BF16)


def land(places, z, refs, held, sems):
    copies = []
    for i, ((far, row), ref) in enumerate(zip(places, refs)):
        at = lax.rem(z + NZ - far, NZ)
        copies.append(
            pltpu.make_async_copy(ref, held.at[at, pl.ds(row, ref.shape[0])], sems.at[i])
        )
    return copies


def attend_kernel(places, where_ref, starts_ref, q_mine_ref, q_other_ref, *rest):
    n = len(places)
    kv_refs, (mine_ref, other_ref, kv, sems) = rest[:n], rest[n:]
    z, y, k = where_ref[0], where_ref[1], where_ref[2]
    scale = math.log2(math.e) * HS**-0.5
    copies = land(places, z, kv_refs, kv, sems)
    for copy in copies:
        copy.start()
    for ref in (mine_ref, other_ref):
        ref[...] = jnp.zeros_like(ref)
        ref[HS : HS + 1, :] = jnp.full((1, HEADS * ROWS), NEG, F32)
    for copy in copies:
        copy.wait()

    for tile, (q_ref, acc_ref) in enumerate(((q_mine_ref, mine_ref), (q_other_ref, other_ref))):
        core = k if tile == 0 else 1 - k
        q_at = ((z * NY + y) * NC + core) * ROWS
        first, last = where_ref[3 + 2 * tile], where_ref[4 + 2 * tile]
        starts = starts_ref[tile : tile + 1, :]

        def block(plane, j, masked):
            k_at = ((plane * NY + lax.rem(y + j, NY)) * NC + k) * ROWS
            keys = kv[plane, 2 * j * ROWS : (2 * j + 1) * ROWS, :]
            values = kv[plane, (2 * j + 1) * ROWS : (2 * j + 2) * ROWS, :]
            if masked:
                key_pos = k_at + lax.broadcasted_iota(jnp.int32, (ROWS, ROWS), 0)
                query_pos = q_at + lax.broadcasted_iota(jnp.int32, (ROWS, ROWS), 1)
                kept = (key_pos <= query_pos) & (key_pos >= starts)
            ats = [slice(h * ROWS, (h + 1) * ROWS) for h in range(HEADS)]
            ss = [jnp.dot(keys, q_ref[:, at], preferred_element_type=F32) for at in ats]
            vt = values.T
            ws = []
            for at, s in zip(ats, ss):
                if masked:
                    s = jnp.where(kept, s, NEG)
                old = acc_ref[HS : HS + 1, at]
                top = jnp.maximum(old, jnp.max(s, axis=0, keepdims=True) * scale)
                w = jnp.exp2(s * scale - top)
                fade = jnp.exp2(old - top)
                acc_ref[HS : HS + 1, at] = top
                acc_ref[HS + 1 : HS + 2, at] = acc_ref[HS + 1 : HS + 2, at] * fade + jnp.sum(
                    w, axis=0, keepdims=True
                )
                ws.append((fade, w.astype(BF16)))
            for at, (fade, w) in zip(ats, ws):
                acc_ref[:HS, at] = acc_ref[:HS, at] * fade + jnp.dot(vt, w, preferred_element_type=F32)

        def wide(plane):
            ats = [slice(h * ROWS, (h + 1) * ROWS) for h in range(HEADS)]
            k0, k1 = kv[plane, :ROWS, :], kv[plane, 2 * ROWS : 3 * ROWS, :]
            ss = [
                (
                    jnp.dot(k0, q_ref[:, at], preferred_element_type=F32),
                    jnp.dot(k1, q_ref[:, at], preferred_element_type=F32),
                )
                for at in ats
            ]
            vt = jnp.concatenate([kv[plane, ROWS : 2 * ROWS, :], kv[plane, 3 * ROWS :, :]]).T
            ws = []
            for at, (s0, s1) in zip(ats, ss):
                old = acc_ref[HS : HS + 1, at]
                top = jnp.maximum(old, jnp.max(jnp.maximum(s0, s1), axis=0, keepdims=True) * scale)
                w0 = jnp.exp2(s0 * scale - top)
                w1 = jnp.exp2(s1 * scale - top)
                fade = jnp.exp2(old - top)
                acc_ref[HS : HS + 1, at] = top
                acc_ref[HS + 1 : HS + 2, at] = acc_ref[HS + 1 : HS + 2, at] * fade + jnp.sum(
                    w0 + w1, axis=0, keepdims=True
                )
                ws.append((fade, jnp.concatenate([w0.astype(BF16), w1.astype(BF16)])))
            for at, (fade, w) in zip(ats, ws):
                acc_ref[:HS, at] = acc_ref[:HS, at] * fade + jnp.dot(vt, w, preferred_element_type=F32)

        @pl.loop(0, NZ)
        def _(plane):
            low = plane * NY * NC * ROWS
            high = ((plane * NY + 1) * NC + k) * ROWS
            clear = (high < q_at) & (low >= last)

            @pl.when(clear)
            def _():
                wide(plane)

            for j in range(NY):
                k_at = ((plane * NY + lax.rem(y + j, NY)) * NC + k) * ROWS
                needed = (k_at <= q_at) & (k_at + ROWS > first) & jnp.logical_not(clear)
                whole = (k_at < q_at) & (k_at >= last)

                @pl.when(needed & whole)
                def _():
                    block(plane, j, False)

                @pl.when(needed & jnp.logical_not(whole))
                def _():
                    block(plane, j, True)


def project_kernel(mine_ref, came_ref, w_ref, out_ref, weights, att, sems):
    def copy(c):
        part = pl.ds(c * COLS, COLS)
        return pltpu.make_async_copy(w_ref.at[:, part], weights.at[c], sems.at[c])

    for c in range(NTP):
        copy(c).start()
    for h in range(HEADS):
        at = slice(h * ROWS, (h + 1) * ROWS)
        a, b = mine_ref[HS : HS + 1, at], came_ref[HS : HS + 1, at]
        top = jnp.maximum(a, b)
        fa, fb = jnp.exp2(a - top), jnp.exp2(b - top)
        weight_sum = mine_ref[HS + 1 : HS + 2, at] * fa + came_ref[HS + 1 : HS + 2, at] * fb
        blended = (mine_ref[:HS, at] * fa + came_ref[:HS, at] * fb) / weight_sum
        att[:, h * HS : (h + 1) * HS] = blended.T.astype(BF16)
    for c in range(NTP):
        copy(c).wait()
        out_ref[c] = jnp.dot(att[...], weights[c], preferred_element_type=F32).astype(BF16)


def gram_part(acc, rows, cols):
    acc[...] += jnp.dot(rows, cols, preferred_element_type=F32)


def add_sums(rows, row_sum, cols, col_sum):
    wide = rows.astype(F32)
    row_sum[...] += sum(wide[:, at : at + HS] for at in range(0, rows.shape[1], HS))
    col_sum[0:1, :] += jnp.sum(cols.astype(F32), axis=0, keepdims=True)


def gram_in_kernel(places, where_ref, rows_ref, *args):
    n = len(places)
    refs, (acc, row_sum, col_sum, rows, cols, sems) = args[:n], args[n:]
    z = where_ref[0]
    for far in range(NZ):
        here = lax.rem(2 * z + NZ - far, NTP)
        pltpu.make_async_copy(rows_ref.at[here], rows.at[far], sems.at[0, far]).start()
    for (far, row), ref in zip(places, refs):
        to = cols.at[far, pl.ds(row, ref.shape[0])]
        pltpu.make_async_copy(ref, to, sems.at[1, far]).start()
    for ref in (acc, row_sum, col_sum):
        ref[...] = jnp.zeros_like(ref)

    @pl.loop(0, NZ)
    def _(far):
        pltpu.make_async_copy(rows_ref.at[0], rows.at[far], sems.at[0, far]).wait()
        pltpu.make_async_copy(cols.at[far], cols.at[far], sems.at[1, far]).wait()
        gram_part(acc, rows[far], cols[far])
        add_sums(rows[far], row_sum, cols[far], col_sum)


def gram_kernel(places, *args):
    where_ref, rows_in_ref, rows_out_ref, cols_in_ref, ii, row_sum_in, col_sum_in = args[:7]
    args, n = args[7:], len(places)
    refs, (mine_ref, other_ref) = args[:n], args[n : n + 2]
    rows_in, rows_out, cols_in, cols_out, io, oi, oo, row_sum, col_sum, sems = args[n + 2 :]
    z, k = where_ref[0], where_ref[2]

    def copies(far):
        here = lax.rem(2 * z + NZ - far, NTP)
        return (
            pltpu.make_async_copy(rows_out_ref.at[here], rows_out.at[far], sems.at[0, far]),
            pltpu.make_async_copy(rows_in_ref.at[far], rows_in.at[far], sems.at[1, far]),
            pltpu.make_async_copy(cols_in_ref.at[far], cols_in.at[far], sems.at[2, far]),
        )

    def block_copies(far):
        for (at, row), ref in zip(places, refs):
            if at == far:
                to = cols_out.at[far, pl.ds(row, ref.shape[0])]
                pltpu.make_async_copy(ref, to, sems.at[3, far]).start()

    ahead = 2
    for far in range(ahead):
        for copy in copies(far):
            copy.start()
        block_copies(far)
    for ref in (io, oi, oo, row_sum, col_sum):
        ref[...] = jnp.zeros_like(ref)

    @pl.loop(0, NZ)
    def _(far):
        @pl.when(far + ahead < NZ)
        def _():
            for copy in copies(far + ahead):
                copy.start()

        for later in range(ahead, NZ):

            @pl.when(far + ahead == later)
            def _():
                block_copies(later)

        for copy in copies(far):
            copy.wait()
        pltpu.make_async_copy(cols_out.at[far], cols_out.at[far], sems.at[3, far]).wait()
        gram_part(io, rows_in[far], cols_out[far])
        gram_part(oi, rows_out[far], cols_in[far])
        gram_part(oo, rows_out[far], cols_out[far])
        add_sums(rows_out[far], row_sum, cols_out[far], col_sum)

    for core, ref in ((k, mine_ref), (1 - k, other_ref)):
        rows = pl.ds(pl.multiple_of(core * HS, HS), HS)
        for at, (left, right, sums) in ((0, (ii, io, row_sum_in)), (HS, (oi, oo, row_sum))):
            ref[at : at + HS, :COLS] = left[rows, :]
            ref[at : at + HS, COLS : 2 * COLS] = right[rows, :]
            ref[at : at + HS, 2 * COLS :] = sums[rows, :]
        ref[2 * HS :, :COLS] = col_sum_in[...]
        ref[2 * HS :, COLS : 2 * COLS] = col_sum[...]
        ref[2 * HS :, 2 * COLS :] = jnp.zeros((8, HS), F32)


def finish_kernel(tokens, mine_ref, came_ref, out_ref):
    col_mean = (mine_ref[2 * HS :, :] + came_ref[2 * HS :, :])[0:1, : 2 * COLS] / tokens
    row_sums = mine_ref[: 2 * HS, 2 * COLS :] + came_ref[: 2 * HS, 2 * COLS :]
    row_mean = jnp.sum(row_sums, axis=1, keepdims=True) / tokens
    for a in range(2):
        for b in range(2):
            rows, cols = slice(a * HS, (a + 1) * HS), slice(b * COLS, (b + 1) * COLS)
            gram = mine_ref[rows, cols] + came_ref[rows, cols]
            out_ref[a, :, b, :] = gram / tokens - row_mean[rows, :] * col_mean[:, cols]


def on_device(hidden_in, norm_gain, w_query, w_key, w_value, w_out, doc_ids):
    tok_index = lax.axis_index("tok")
    z, y, k = tok_index // (NY * NC), (tok_index // NC) % NY, tok_index % NC
    tokens = ROWS * NZ * NY * NC

    first_row = tok_index * ROWS
    other_row = (tok_index + 1 - 2 * k) * ROWS
    doc_start = jnp.stack([jnp.sum((doc_ids < d).astype(jnp.int32)) for d in range(4)])

    def starts_of(row):
        docs = lax.dynamic_slice_in_dim(doc_ids, row, ROWS, 0)
        return sum(jnp.where(docs == d, doc_start[d], 0) for d in range(4))

    starts = jnp.stack([starts_of(first_row), starts_of(other_row)])
    place = jnp.stack([z, y, k]).astype(jnp.int32)
    ends = jnp.stack([starts[0, 0], starts[0, -1], starts[1, 0], starts[1, -1]])
    where = jnp.concatenate([place, ends]).astype(jnp.int32)
    inv_freq = ROPE_BASE ** (-(jnp.arange(HS // 2, dtype=F32) * 2.0) / HS)
    positions = first_row + jnp.arange(ROWS, dtype=jnp.int32)
    angles = positions.astype(F32)[:, None] * inv_freq[None, :]
    cosine, sine = jnp.cos(angles), jnp.sin(angles)
    cos = jnp.concatenate([cosine, cosine], axis=1)
    sin = jnp.concatenate([-sine, sine], axis=1)

    def rows_in_plane(x):
        here = lax.dynamic_slice_in_dim(x, y * HALF, HALF, 1).T
        there = lax.dynamic_slice_in_dim(x, (1 - y) * HALF, HALF, 1).T
        here = lax.ppermute(here, BOTH, IN_PLANE)
        there = lax.ppermute(there, BOTH, IN_PLANE_OTHER_Y)
        return jnp.concatenate([here, there], axis=1)

    full_in = gather_tp(copies_for_tp(hidden_in))
    in_blocks = ring(hidden_in)
    rows_in = rows_in_plane(hidden_in)
    early = [b[2] for b in in_blocks[:-2]]
    full_in = after(full_in, cos, sin, where, starts, rows_in, *early)
    normed, kv = pl.pallas_call(
        norm_kv_kernel,
        out_shape=(
            jax.ShapeDtypeStruct((NTP, ROWS, COLS), BF16),
            jax.ShapeDtypeStruct((2 * ROWS, HS), BF16),
        ),
        in_specs=[VMEM] * 6,
        out_specs=(VMEM, VMEM),
        compiler_params=params(14),
        cost_estimate=cost(1 << 30, 6 << 20),
        name="norm_kv",
    )(full_in, norm_gain.reshape(NTP, COLS), w_key, w_value, cos, sin)
    kv_pair = jnp.concatenate([kv, lax.ppermute(kv, "tok", OTHER_Y)])

    q = pl.pallas_call(
        query_kernel,
        out_shape=jax.ShapeDtypeStruct((HS, HEADS * ROWS), BF16),
        in_specs=[VMEM, ANY, VMEM, VMEM],
        out_specs=VMEM,
        scratch_shapes=[
            pltpu.VMEM((NTP * COLS, HEADS * HS), BF16),
            pltpu.SemaphoreType.DMA((NTP,)),
        ],
        compiler_params=params(60),
        cost_estimate=cost(1 << 30, 6 << 20),
        name="queries",
    )(normed, w_query, cos, sin)
    in_other = lax.ppermute(after(hidden_in, kv), "tok", OTHER_Y)
    moved = lax.ppermute(rows_in, BOTH, TO_PLANE)
    kv_blocks = ring(kv_pair, {3: (moved, q, in_other)})
    rows_in = gather_tp(copies_for_tp(moved))
    q_other = lax.ppermute(q, "tok", OTHER_CORE)

    half = jax.ShapeDtypeStruct((HS + 8, HEADS * ROWS), F32)
    mine, other = pl.pallas_call(
        functools.partial(attend_kernel, [b[:2] for b in kv_blocks]),
        out_shape=(half, half),
        in_specs=[SMEM, VMEM, VMEM, VMEM] + [ANY] * len(kv_blocks),
        out_specs=(VMEM, VMEM),
        scratch_shapes=[
            pltpu.VMEM((NZ, 2 * NY * ROWS, HS), BF16),
            pltpu.SemaphoreType.DMA((len(kv_blocks),)),
        ],
        compiler_params=params(60),
        cost_estimate=cost(16 << 30, 6 << 20),
        name="attend",
    )(where, starts, q, q_other, *[b[2] for b in kv_blocks])
    came = after(lax.ppermute(other, "tok", OTHER_CORE), rows_in)

    partial_out = pl.pallas_call(
        project_kernel,
        out_shape=jax.ShapeDtypeStruct((NTP, ROWS, COLS), BF16),
        in_specs=[VMEM, VMEM, ANY],
        out_specs=VMEM,
        scratch_shapes=[
            pltpu.VMEM((NTP, HEADS * HS, COLS), BF16),
            pltpu.VMEM((ROWS, HEADS * HS), BF16),
            pltpu.SemaphoreType.DMA((NTP,)),
        ],
        compiler_params=params(60),
        cost_estimate=cost(1 << 30, 8 << 20),
        name="project",
    )(mine, came, w_out)
    shares = lax.all_to_all(partial_out, "tp", split_axis=0, concat_axis=0, tiled=True)

    in_blocks = [b[:2] + (after(b[2], other),) for b in in_blocks]
    in_blocks += [(f, ROWS + r, b) for f, r, b in ring(after(in_other, other))]
    part = jax.ShapeDtypeStruct((HALF, COLS), F32)
    ii, row_sum_in, col_sum_in, rows_in, cols_in = pl.pallas_call(
        functools.partial(gram_in_kernel, [b[:2] for b in in_blocks]),
        out_shape=(
            part,
            jax.ShapeDtypeStruct((HALF, HS), F32),
            jax.ShapeDtypeStruct((8, COLS), F32),
            jax.ShapeDtypeStruct((NZ, HALF, NY * ROWS), BF16),
            jax.ShapeDtypeStruct((NZ, NY * ROWS, COLS), BF16),
        ),
        in_specs=[SMEM] + [ANY] * (1 + len(in_blocks)),
        out_specs=(VMEM,) * 5,
        scratch_shapes=[pltpu.SemaphoreType.DMA((2, NZ))],
        compiler_params=params(60),
        cost_estimate=cost(1 << 30, 12 << 20),
        name="gram_in",
    )(where, rows_in, *[b[2] for b in in_blocks])
    shares = after(shares, ii)
    hidden_out = (
        hidden_in.astype(F32) + jnp.sum(shares.astype(F32), axis=0)
    ).astype(BF16)
    rows_out = rows_in_plane(hidden_out)
    out_pair = jnp.concatenate([hidden_out, lax.ppermute(hidden_out, "tok", OTHER_Y)])
    moved = lax.ppermute(rows_out, BOTH, TO_PLANE)
    out_blocks = ring(after(out_pair, rows_out), {2: (moved,)})
    rows_out = gather_tp(copies_for_tp(moved))
    acc = pltpu.VMEM((HALF, COLS), F32)
    half = jax.ShapeDtypeStruct((2 * HS + 8, 2 * COLS + HS), F32)
    mine, other = pl.pallas_call(
        functools.partial(gram_kernel, [b[:2] for b in out_blocks]),
        out_shape=(half, half),
        in_specs=[SMEM] + [ANY] * 3 + [VMEM] * 3 + [ANY] * len(out_blocks),
        out_specs=(VMEM, VMEM),
        scratch_shapes=[
            pltpu.VMEM((NZ, HALF, NY * ROWS), BF16),
            pltpu.VMEM((NZ, HALF, NY * ROWS), BF16),
            pltpu.VMEM((NZ, NY * ROWS, COLS), BF16),
            pltpu.VMEM((NZ, NY * ROWS, COLS), BF16),
            acc,
            acc,
            acc,
            pltpu.VMEM((HALF, HS), F32),
            pltpu.VMEM((8, COLS), F32),
            pltpu.SemaphoreType.DMA((4, NZ)),
        ],
        compiler_params=params(60),
        cost_estimate=cost(6 << 30, 14 << 20),
        name="gram",
    )(
        where,
        rows_in,
        rows_out,
        cols_in,
        ii,
        row_sum_in,
        col_sum_in,
        *[b[2] for b in out_blocks],
    )
    joint_cov = pl.pallas_call(
        functools.partial(finish_kernel, tokens),
        out_shape=jax.ShapeDtypeStruct((2, HS, 2, COLS), F32),
        in_specs=[VMEM, VMEM],
        out_specs=VMEM,
        compiler_params=params(14),
        cost_estimate=cost(1 << 22, 3 << 20),
        name="finish",
    )(mine, lax.ppermute(other, "tok", OTHER_CORE))
    return hidden_out, joint_cov


def solution(mesh):
    return jax.shard_map(
        on_device,
        mesh=mesh,
        in_specs=(
            P("tok", "tp"),
            P(),
            P(None, "tp"),
            P(None, "tp"),
            P(None, "tp"),
            P("tp", None),
            P(),
        ),
        out_specs=(P("tok", "tp"), P(None, "tok", None, "tp")),
        check_vma=False,
    )
```

```python
import functools
import math

import jax
import jax.numpy as jnp
from jax import lax
from jax.experimental import pallas as pl
from jax.experimental.pallas import tpu as pltpu
from jax.sharding import PartitionSpec as P

HS = 128
EPS = 1e-05
ROPE_BASE = 500000.0
NEG = -1e30
F32 = jnp.float32
BF16 = jnp.bfloat16

NZ, NY, NC, NTP = 8, 2, 2, 8
ROWS = 256
COLS = 512
HALF = 256
HEADS = 4
BOTH = ("tok", "tp")
VMEM = pl.BlockSpec(memory_space=pltpu.VMEM)
SMEM = pl.BlockSpec(memory_space=pltpu.SMEM)
ANY = pl.BlockSpec(memory_space=pl.ANY)


def tok_of(z, y, k):
    return (z * NY + y) * NC + k


CELLS = [(z, y, k) for z in range(NZ) for y in range(NY) for k in range(NC)]
UP = [(tok_of(z, y, k), tok_of((z + 1) % NZ, y, k)) for z, y, k in CELLS]
DOWN = [(b, a) for a, b in UP]
OTHER_Y = [(tok_of(z, y, k), tok_of(z, 1 - y, k)) for z, y, k in CELLS]
OTHER_CORE = [(tok_of(z, y, k), tok_of(z, y, 1 - k)) for z, y, k in CELLS]
IN_PLANE = [
    (tok_of(z, y, k) * NTP + c, tok_of(z, y, k) * NTP + (z + c) % NTP)
    for z, y, k in CELLS
    for c in range(NTP)
]
IN_PLANE_OTHER_Y = [
    (tok_of(z, y, k) * NTP + c, tok_of(z, 1 - y, k) * NTP + (z + c) % NTP)
    for z, y, k in CELLS
    for c in range(NTP)
]
TO_PLANE = [
    (tok_of(z, y, k) * NTP + (z + c) % NTP, tok_of(c, y, k) * NTP + (z + c) % NTP)
    for z, y, k in CELLS
    for c in range(NTP)
]


def params(mib, **kw):
    return pltpu.CompilerParams(vmem_limit_bytes=mib << 20, **kw)


def cost(flops, moved):
    return pl.CostEstimate(flops=flops, bytes_accessed=moved, transcendentals=0)


def after(x, *earlier):
    return lax.optimization_barrier((x, *earlier))[0]


def copies_for_tp(x):
    return jnp.broadcast_to(x, (NTP, *x.shape))


def gather_tp(copies):
    return lax.all_to_all(copies, "tp", split_axis=0, concat_axis=0, tiled=True)


def ring(x, meanwhile=()):
    got, up, down = [(0, 0, x)], x, x
    for step in range(1, NZ // 2):
        if step in meanwhile:
            up, down = after(up, *meanwhile[step]), after(down, *meanwhile[step])
        up, down = lax.ppermute(up, "tok", UP), lax.ppermute(down, "tok", DOWN)
        got += [(step, 0, up), (NZ - step, 0, down)]
    middle = x.shape[0] // 2
    got.append((NZ // 2, 0, lax.ppermute(up[:middle], "tok", UP)))
    got.append((NZ // 2, middle, lax.ppermute(down[middle:], "tok", DOWN)))
    return got


def turned(x, cos, sin):
    return x * cos + pltpu.roll(x, HS // 2, 1) * sin


def norm_kv_kernel(x_ref, gain_ref, wk_ref, wv_ref, cos_ref, sin_ref, normed_ref, kv_ref):
    total = jnp.zeros((ROWS, 1), F32)
    for c in range(NTP):
        x = x_ref[c].astype(F32)
        total += jnp.sum(x * x, axis=1, keepdims=True)
    factor = lax.rsqrt(total / (NTP * COLS) + EPS)
    k = jnp.zeros((ROWS, HS), F32)
    v = jnp.zeros((ROWS, HS), F32)
    for c in range(NTP):
        normed = (x_ref[c].astype(F32) * factor * gain_ref[c : c + 1, :]).astype(BF16)
        normed_ref[c] = normed
        k += jnp.dot(normed, wk_ref[c * COLS : (c + 1) * COLS, :], preferred_element_type=F32)
        v += jnp.dot(normed, wv_ref[c * COLS : (c + 1) * COLS, :], preferred_element_type=F32)
    kv_ref[:ROWS, :] = turned(k, cos_ref[...], sin_ref[...]).astype(BF16)
    kv_ref[ROWS:, :] = v.astype(BF16)


def query_kernel(normed_ref, wq_ref, cos_ref, sin_ref, q_ref, weights, sems):
    def copy(c):
        part = pl.ds(c * COLS, COLS)
        return pltpu.make_async_copy(wq_ref.at[part], weights.at[part], sems.at[c])

    for c in range(NTP):
        copy(c).start()
    acc = jnp.zeros((ROWS, HEADS * HS), F32)
    for c in range(NTP):
        copy(c).wait()
        part = weights[c * COLS : (c + 1) * COLS, :]
        acc += jnp.dot(normed_ref[c], part, preferred_element_type=F32)
    for h in range(HEADS):
        q = turned(acc[:, h * HS : (h + 1) * HS], cos_ref[...], sin_ref[...])
        q_ref[:, h * ROWS : (h + 1) * ROWS] = q.T.astype(BF16)


def land(places, z, refs, held, sems):
    copies = []
    for i, ((far, row), ref) in enumerate(zip(places, refs)):
        at = lax.rem(z + NZ - far, NZ)
        copies.append(
            pltpu.make_async_copy(ref, held.at[at, pl.ds(row, ref.shape[0])], sems.at[i])
        )
    return copies


def attend_kernel(places, where_ref, starts_ref, q_mine_ref, q_other_ref, *rest):
    n = len(places)
    kv_refs, (mine_ref, other_ref, kv, sems) = rest[:n], rest[n:]
    z, y, k = where_ref[0], where_ref[1], where_ref[2]
    scale = math.log2(math.e) * HS**-0.5
    copies = land(places, z, kv_refs, kv, sems)
    for copy in copies:
        copy.start()
    for ref in (mine_ref, other_ref):
        ref[...] = jnp.zeros_like(ref)
        ref[HS : HS + 1, :] = jnp.full((1, HEADS * ROWS), NEG, F32)
    for copy in copies:
        copy.wait()

    for tile, (q_ref, acc_ref) in enumerate(((q_mine_ref, mine_ref), (q_other_ref, other_ref))):
        core = k if tile == 0 else 1 - k
        q_at = ((z * NY + y) * NC + core) * ROWS
        first, last = where_ref[3 + 2 * tile], where_ref[4 + 2 * tile]
        starts = starts_ref[tile : tile + 1, :]

        def block(plane, j, masked):
            k_at = ((plane * NY + lax.rem(y + j, NY)) * NC + k) * ROWS
            keys = kv[plane, 2 * j * ROWS : (2 * j + 1) * ROWS, :]
            values = kv[plane, (2 * j + 1) * ROWS : (2 * j + 2) * ROWS, :]
            if masked:
                key_pos = k_at + lax.broadcasted_iota(jnp.int32, (ROWS, ROWS), 0)
                query_pos = q_at + lax.broadcasted_iota(jnp.int32, (ROWS, ROWS), 1)
                kept = (key_pos <= query_pos) & (key_pos >= starts)
            ats = [slice(h * ROWS, (h + 1) * ROWS) for h in range(HEADS)]
            ss = [jnp.dot(keys, q_ref[:, at], preferred_element_type=F32) for at in ats]
            vt = values.T
            ws = []
            for at, s in zip(ats, ss):
                if masked:
                    s = jnp.where(kept, s, NEG)
                old = acc_ref[HS : HS + 1, at]
                top = jnp.maximum(old, jnp.max(s, axis=0, keepdims=True) * scale)
                w = jnp.exp2(s * scale - top)
                fade = jnp.exp2(old - top)
                acc_ref[HS : HS + 1, at] = top
                acc_ref[HS + 1 : HS + 2, at] = acc_ref[HS + 1 : HS + 2, at] * fade + jnp.sum(
                    w, axis=0, keepdims=True
                )
                ws.append((fade, w.astype(BF16)))
            for at, (fade, w) in zip(ats, ws):
                acc_ref[:HS, at] = acc_ref[:HS, at] * fade + jnp.dot(vt, w, preferred_element_type=F32)

        def wide(plane):
            ats = [slice(h * ROWS, (h + 1) * ROWS) for h in range(HEADS)]
            k0, k1 = kv[plane, :ROWS, :], kv[plane, 2 * ROWS : 3 * ROWS, :]
            ss = [
                (
                    jnp.dot(k0, q_ref[:, at], preferred_element_type=F32),
                    jnp.dot(k1, q_ref[:, at], preferred_element_type=F32),
                )
                for at in ats
            ]
            vt = jnp.concatenate([kv[plane, ROWS : 2 * ROWS, :], kv[plane, 3 * ROWS :, :]]).T
            ws = []
            for at, (s0, s1) in zip(ats, ss):
                old = acc_ref[HS : HS + 1, at]
                top = jnp.maximum(old, jnp.max(jnp.maximum(s0, s1), axis=0, keepdims=True) * scale)
                w0 = jnp.exp2(s0 * scale - top)
                w1 = jnp.exp2(s1 * scale - top)
                fade = jnp.exp2(old - top)
                acc_ref[HS : HS + 1, at] = top
                acc_ref[HS + 1 : HS + 2, at] = acc_ref[HS + 1 : HS + 2, at] * fade + jnp.sum(
                    w0 + w1, axis=0, keepdims=True
                )
                ws.append((fade, jnp.concatenate([w0.astype(BF16), w1.astype(BF16)])))
            for at, (fade, w) in zip(ats, ws):
                acc_ref[:HS, at] = acc_ref[:HS, at] * fade + jnp.dot(vt, w, preferred_element_type=F32)

        @pl.loop(0, NZ)
        def _(plane):
            low = plane * NY * NC * ROWS
            high = ((plane * NY + 1) * NC + k) * ROWS
            clear = (high < q_at) & (low >= last)

            @pl.when(clear)
            def _():
                wide(plane)

            for j in range(NY):
                k_at = ((plane * NY + lax.rem(y + j, NY)) * NC + k) * ROWS
                needed = (k_at <= q_at) & (k_at + ROWS > first) & jnp.logical_not(clear)
                whole = (k_at < q_at) & (k_at >= last)

                @pl.when(needed & whole)
                def _():
                    block(plane, j, False)

                @pl.when(needed & jnp.logical_not(whole))
                def _():
                    block(plane, j, True)


def project_kernel(mine_ref, came_ref, w_ref, out_ref, weights, att, sems):
    def copy(c):
        part = pl.ds(c * COLS, COLS)
        return pltpu.make_async_copy(w_ref.at[:, part], weights.at[c], sems.at[c])

    for c in range(NTP):
        copy(c).start()
    for h in range(HEADS):
        at = slice(h * ROWS, (h + 1) * ROWS)
        a, b = mine_ref[HS : HS + 1, at], came_ref[HS : HS + 1, at]
        top = jnp.maximum(a, b)
        fa, fb = jnp.exp2(a - top), jnp.exp2(b - top)
        weight_sum = mine_ref[HS + 1 : HS + 2, at] * fa + came_ref[HS + 1 : HS + 2, at] * fb
        blended = (mine_ref[:HS, at] * fa + came_ref[:HS, at] * fb) / weight_sum
        att[:, h * HS : (h + 1) * HS] = blended.T.astype(BF16)
    for c in range(NTP):
        copy(c).wait()
        out_ref[c] = jnp.dot(att[...], weights[c], preferred_element_type=F32).astype(BF16)


def gram_part(acc, rows, cols):
    acc[...] += jnp.dot(rows, cols, preferred_element_type=F32)


def add_sums(rows, row_sum, cols, col_sum):
    wide = rows.astype(F32)
    row_sum[...] += sum(wide[:, at : at + HS] for at in range(0, rows.shape[1], HS))
    col_sum[0:1, :] += jnp.sum(cols.astype(F32), axis=0, keepdims=True)


def gram_in_kernel(places, where_ref, rows_ref, *args):
    n = len(places)
    refs, (acc, row_sum, col_sum, rows, cols, sems) = args[:n], args[n:]
    z = where_ref[0]
    for far in range(NZ):
        here = lax.rem(2 * z + NZ - far, NTP)
        pltpu.make_async_copy(rows_ref.at[here], rows.at[far], sems.at[0, far]).start()
    for (far, row), ref in zip(places, refs):
        to = cols.at[far, pl.ds(row, ref.shape[0])]
        pltpu.make_async_copy(ref, to, sems.at[1, far]).start()
    for ref in (acc, row_sum, col_sum):
        ref[...] = jnp.zeros_like(ref)

    @pl.loop(0, NZ)
    def _(far):
        pltpu.make_async_copy(rows_ref.at[0], rows.at[far], sems.at[0, far]).wait()
        pltpu.make_async_copy(cols.at[far], cols.at[far], sems.at[1, far]).wait()
        gram_part(acc, rows[far], cols[far])
        add_sums(rows[far], row_sum, cols[far], col_sum)


def gram_kernel(places, *args):
    where_ref, rows_in_ref, rows_out_ref, cols_in_ref, ii, row_sum_in, col_sum_in = args[:7]
    args, n = args[7:], len(places)
    refs, (mine_ref, other_ref) = args[:n], args[n : n + 2]
    rows_in, rows_out, cols_in, cols_out, io, oi, oo, row_sum, col_sum, sems = args[n + 2 :]
    z, k = where_ref[0], where_ref[2]

    def copies(far):
        here = lax.rem(2 * z + NZ - far, NTP)
        return (
            pltpu.make_async_copy(rows_out_ref.at[here], rows_out.at[far], sems.at[0, far]),
            pltpu.make_async_copy(rows_in_ref.at[far], rows_in.at[far], sems.at[1, far]),
            pltpu.make_async_copy(cols_in_ref.at[far], cols_in.at[far], sems.at[2, far]),
        )

    def block_copies(far):
        for (at, row), ref in zip(places, refs):
            if at == far:
                to = cols_out.at[far, pl.ds(row, ref.shape[0])]
                pltpu.make_async_copy(ref, to, sems.at[3, far]).start()

    ahead = 2
    for far in range(ahead):
        for copy in copies(far):
            copy.start()
        block_copies(far)
    for ref in (io, oi, oo, row_sum, col_sum):
        ref[...] = jnp.zeros_like(ref)

    @pl.loop(0, NZ)
    def _(far):
        @pl.when(far + ahead < NZ)
        def _():
            for copy in copies(far + ahead):
                copy.start()

        for later in range(ahead, NZ):

            @pl.when(far + ahead == later)
            def _():
                block_copies(later)

        for copy in copies(far):
            copy.wait()
        pltpu.make_async_copy(cols_out.at[far], cols_out.at[far], sems.at[3, far]).wait()
        gram_part(io, rows_in[far], cols_out[far])
        gram_part(oi, rows_out[far], cols_in[far])
        gram_part(oo, rows_out[far], cols_out[far])
        add_sums(rows_out[far], row_sum, cols_out[far], col_sum)

    for core, ref in ((k, mine_ref), (1 - k, other_ref)):
        rows = pl.ds(pl.multiple_of(core * HS, HS), HS)
        for at, (left, right, sums) in ((0, (ii, io, row_sum_in)), (HS, (oi, oo, row_sum))):
            ref[at : at + HS, :COLS] = left[rows, :]
            ref[at : at + HS, COLS : 2 * COLS] = right[rows, :]
            ref[at : at + HS, 2 * COLS :] = sums[rows, :]
        ref[2 * HS :, :COLS] = col_sum_in[...]
        ref[2 * HS :, COLS : 2 * COLS] = col_sum[...]
        ref[2 * HS :, 2 * COLS :] = jnp.zeros((8, HS), F32)


def finish_kernel(tokens, mine_ref, came_ref, out_ref):
    col_mean = (mine_ref[2 * HS :, :] + came_ref[2 * HS :, :])[0:1, : 2 * COLS] / tokens
    row_sums = mine_ref[: 2 * HS, 2 * COLS :] + came_ref[: 2 * HS, 2 * COLS :]
    row_mean = jnp.sum(row_sums, axis=1, keepdims=True) / tokens
    for a in range(2):
        for b in range(2):
            rows, cols = slice(a * HS, (a + 1) * HS), slice(b * COLS, (b + 1) * COLS)
            gram = mine_ref[rows, cols] + came_ref[rows, cols]
            out_ref[a, :, b, :] = gram / tokens - row_mean[rows, :] * col_mean[:, cols]


def on_device(hidden_in, norm_gain, w_query, w_key, w_value, w_out, doc_ids):
    tok_index = lax.axis_index("tok")
    z, y, k = tok_index // (NY * NC), (tok_index // NC) % NY, tok_index % NC
    tokens = ROWS * NZ * NY * NC

    first_row = tok_index * ROWS
    other_row = (tok_index + 1 - 2 * k) * ROWS
    doc_start = jnp.stack([jnp.sum((doc_ids < d).astype(jnp.int32)) for d in range(4)])

    def starts_of(row):
        docs = lax.dynamic_slice_in_dim(doc_ids, row, ROWS, 0)
        return sum(jnp.where(docs == d, doc_start[d], 0) for d in range(4))

    starts = jnp.stack([starts_of(first_row), starts_of(other_row)])
    place = jnp.stack([z, y, k]).astype(jnp.int32)
    ends = jnp.stack([starts[0, 0], starts[0, -1], starts[1, 0], starts[1, -1]])
    where = jnp.concatenate([place, ends]).astype(jnp.int32)
    inv_freq = ROPE_BASE ** (-(jnp.arange(HS // 2, dtype=F32) * 2.0) / HS)
    positions = first_row + jnp.arange(ROWS, dtype=jnp.int32)
    angles = positions.astype(F32)[:, None] * inv_freq[None, :]
    cosine, sine = jnp.cos(angles), jnp.sin(angles)
    cos = jnp.concatenate([cosine, cosine], axis=1)
    sin = jnp.concatenate([-sine, sine], axis=1)

    def rows_in_plane(x):
        here = lax.dynamic_slice_in_dim(x, y * HALF, HALF, 1).T
        there = lax.dynamic_slice_in_dim(x, (1 - y) * HALF, HALF, 1).T
        here = lax.ppermute(here, BOTH, IN_PLANE)
        there = lax.ppermute(there, BOTH, IN_PLANE_OTHER_Y)
        return jnp.concatenate([here, there], axis=1)

    full_in = gather_tp(copies_for_tp(hidden_in))
    in_blocks = ring(hidden_in)
    rows_in = rows_in_plane(hidden_in)
    early = [b[2] for b in in_blocks]
    full_in = after(full_in, cos, sin, where, starts, rows_in, *early)
    normed, kv = pl.pallas_call(
        norm_kv_kernel,
        out_shape=(
            jax.ShapeDtypeStruct((NTP, ROWS, COLS), BF16),
            jax.ShapeDtypeStruct((2 * ROWS, HS), BF16),
        ),
        in_specs=[VMEM] * 6,
        out_specs=(VMEM, VMEM),
        compiler_params=params(14),
        cost_estimate=cost(1 << 30, 6 << 20),
        name="norm_kv",
    )(full_in, norm_gain.reshape(NTP, COLS), w_key, w_value, cos, sin)
    kv_pair = jnp.concatenate([kv, lax.ppermute(kv, "tok", OTHER_Y)])

    q = pl.pallas_call(
        query_kernel,
        out_shape=jax.ShapeDtypeStruct((HS, HEADS * ROWS), BF16),
        in_specs=[VMEM, ANY, VMEM, VMEM],
        out_specs=VMEM,
        scratch_shapes=[
            pltpu.VMEM((NTP * COLS, HEADS * HS), BF16),
            pltpu.SemaphoreType.DMA((NTP,)),
        ],
        compiler_params=params(60),
        cost_estimate=cost(1 << 30, 6 << 20),
        name="queries",
    )(normed, w_query, cos, sin)
    in_other = lax.ppermute(after(hidden_in, kv), "tok", OTHER_Y)
    moved = lax.ppermute(rows_in, BOTH, TO_PLANE)
    kv_blocks = ring(kv_pair, {3: (moved, q, in_other)})
    rows_in = gather_tp(copies_for_tp(after(moved, kv_blocks[5][2], kv_blocks[6][2])))
    other_blocks = ring(after(in_other, kv_blocks[5][2]))
    q_other = lax.ppermute(q, "tok", OTHER_CORE)

    half = jax.ShapeDtypeStruct((HS + 8, HEADS * ROWS), F32)
    mine, other = pl.pallas_call(
        functools.partial(attend_kernel, [b[:2] for b in kv_blocks]),
        out_shape=(half, half),
        in_specs=[SMEM, VMEM, VMEM, VMEM] + [ANY] * len(kv_blocks),
        out_specs=(VMEM, VMEM),
        scratch_shapes=[
            pltpu.VMEM((NZ, 2 * NY * ROWS, HS), BF16),
            pltpu.SemaphoreType.DMA((len(kv_blocks),)),
        ],
        compiler_params=params(60),
        cost_estimate=cost(16 << 30, 6 << 20),
        name="attend",
    )(where, starts, q, q_other, *[b[2] for b in kv_blocks])
    came = lax.ppermute(other, "tok", OTHER_CORE)

    partial_out = pl.pallas_call(
        project_kernel,
        out_shape=jax.ShapeDtypeStruct((NTP, ROWS, COLS), BF16),
        in_specs=[VMEM, VMEM, ANY],
        out_specs=VMEM,
        scratch_shapes=[
            pltpu.VMEM((NTP, HEADS * HS, COLS), BF16),
            pltpu.VMEM((ROWS, HEADS * HS), BF16),
            pltpu.SemaphoreType.DMA((NTP,)),
        ],
        compiler_params=params(60),
        cost_estimate=cost(1 << 30, 8 << 20),
        name="project",
    )(mine, came, w_out)
    shares = lax.all_to_all(partial_out, "tp", split_axis=0, concat_axis=0, tiled=True)

    shares = after(shares, rows_in, *[b[2] for b in other_blocks])
    hidden_out = (
        hidden_in.astype(F32) + jnp.sum(shares.astype(F32), axis=0)
    ).astype(BF16)

    rows_out = rows_in_plane(hidden_out)
    out_pair = jnp.concatenate([hidden_out, lax.ppermute(hidden_out, "tok", OTHER_Y)])
    moved = lax.ppermute(rows_out, BOTH, TO_PLANE)
    in_blocks += [(f, ROWS + r, b) for f, r, b in other_blocks]
    part = jax.ShapeDtypeStruct((HALF, COLS), F32)
    ii, row_sum_in, col_sum_in, rows_in, cols_in = pl.pallas_call(
        functools.partial(gram_in_kernel, [b[:2] for b in in_blocks]),
        out_shape=(
            part,
            jax.ShapeDtypeStruct((HALF, HS), F32),
            jax.ShapeDtypeStruct((8, COLS), F32),
            jax.ShapeDtypeStruct((NZ, HALF, NY * ROWS), BF16),
            jax.ShapeDtypeStruct((NZ, NY * ROWS, COLS), BF16),
        ),
        in_specs=[SMEM] + [ANY] * (1 + len(in_blocks)),
        out_specs=(VMEM,) * 5,
        scratch_shapes=[pltpu.SemaphoreType.DMA((2, NZ))],
        compiler_params=params(60),
        cost_estimate=cost(1 << 30, 12 << 20),
        name="gram_in",
    )(where, rows_in, *[b[2] for b in in_blocks])
    out_blocks = ring(after(out_pair, rows_out), {2: (moved,), 3: (ii,)})
    rows_out = gather_tp(copies_for_tp(moved))
    acc = pltpu.VMEM((HALF, COLS), F32)
    half = jax.ShapeDtypeStruct((2 * HS + 8, 2 * COLS + HS), F32)
    mine, other = pl.pallas_call(
        functools.partial(gram_kernel, [b[:2] for b in out_blocks]),
        out_shape=(half, half),
        in_specs=[SMEM] + [ANY] * 3 + [VMEM] * 3 + [ANY] * len(out_blocks),
        out_specs=(VMEM, VMEM),
        scratch_shapes=[
            pltpu.VMEM((NZ, HALF, NY * ROWS), BF16),
            pltpu.VMEM((NZ, HALF, NY * ROWS), BF16),
            pltpu.VMEM((NZ, NY * ROWS, COLS), BF16),
            pltpu.VMEM((NZ, NY * ROWS, COLS), BF16),
            acc,
            acc,
            acc,
            pltpu.VMEM((HALF, HS), F32),
            pltpu.VMEM((8, COLS), F32),
            pltpu.SemaphoreType.DMA((4, NZ)),
        ],
        compiler_params=params(60),
        cost_estimate=cost(6 << 30, 14 << 20),
        name="gram",
    )(
        where,
        rows_in,
        rows_out,
        cols_in,
        ii,
        row_sum_in,
        col_sum_in,
        *[b[2] for b in out_blocks],
    )
    joint_cov = pl.pallas_call(
        functools.partial(finish_kernel, tokens),
        out_shape=jax.ShapeDtypeStruct((2, HS, 2, COLS), F32),
        in_specs=[VMEM, VMEM],
        out_specs=VMEM,
        compiler_params=params(14),
        cost_estimate=cost(1 << 22, 3 << 20),
        name="finish",
    )(mine, lax.ppermute(other, "tok", OTHER_CORE))
    return hidden_out, joint_cov


def solution(mesh):
    return jax.shard_map(
        on_device,
        mesh=mesh,
        in_specs=(
            P("tok", "tp"),
            P(),
            P(None, "tp"),
            P(None, "tp"),
            P(None, "tp"),
            P("tp", None),
            P(),
        ),
        out_specs=(P("tok", "tp"), P(None, "tok", None, "tp")),
        check_vma=False,
    )
```

```python
import functools
import math

import jax
import jax.numpy as jnp
from jax import lax
from jax.experimental import pallas as pl
from jax.experimental.pallas import tpu as pltpu
from jax.sharding import PartitionSpec as P

HS = 128
EPS = 1e-05
ROPE_BASE = 500000.0
NEG = -1e30
F32 = jnp.float32
BF16 = jnp.bfloat16

NZ, NY, NC, NTP = 8, 2, 2, 8
ROWS = 256
COLS = 512
HALF = 256
HEADS = 4
BOTH = ("tok", "tp")
VMEM = pl.BlockSpec(memory_space=pltpu.VMEM)
SMEM = pl.BlockSpec(memory_space=pltpu.SMEM)
ANY = pl.BlockSpec(memory_space=pl.ANY)


def tok_of(z, y, k):
    return (z * NY + y) * NC + k


CELLS = [(z, y, k) for z in range(NZ) for y in range(NY) for k in range(NC)]
UP = [(tok_of(z, y, k), tok_of((z + 1) % NZ, y, k)) for z, y, k in CELLS]
DOWN = [(b, a) for a, b in UP]
OTHER_Y = [(tok_of(z, y, k), tok_of(z, 1 - y, k)) for z, y, k in CELLS]
OTHER_CORE = [(tok_of(z, y, k), tok_of(z, y, 1 - k)) for z, y, k in CELLS]
IN_PLANE = [
    (tok_of(z, y, k) * NTP + c, tok_of(z, y, k) * NTP + (z + c) % NTP)
    for z, y, k in CELLS
    for c in range(NTP)
]
IN_PLANE_OTHER_Y = [
    (tok_of(z, y, k) * NTP + c, tok_of(z, 1 - y, k) * NTP + (z + c) % NTP)
    for z, y, k in CELLS
    for c in range(NTP)
]
TO_PLANE = [
    (tok_of(z, y, k) * NTP + (z + c) % NTP, tok_of(c, y, k) * NTP + (z + c) % NTP)
    for z, y, k in CELLS
    for c in range(NTP)
]


def params(mib, **kw):
    return pltpu.CompilerParams(vmem_limit_bytes=mib << 20, **kw)


def cost(flops, moved):
    return pl.CostEstimate(flops=flops, bytes_accessed=moved, transcendentals=0)


def after(x, *earlier):
    return lax.optimization_barrier((x, *earlier))[0]


def copies_for_tp(x):
    return jnp.broadcast_to(x, (NTP, *x.shape))


def gather_tp(copies):
    return lax.all_to_all(copies, "tp", split_axis=0, concat_axis=0, tiled=True)


def ring(x, meanwhile=()):
    got, up, down = [(0, 0, x)], x, x
    for step in range(1, NZ // 2):
        if step in meanwhile:
            up, down = after(up, *meanwhile[step]), after(down, *meanwhile[step])
        up, down = lax.ppermute(up, "tok", UP), lax.ppermute(down, "tok", DOWN)
        got += [(step, 0, up), (NZ - step, 0, down)]
    middle = x.shape[0] // 2
    got.append((NZ // 2, 0, lax.ppermute(up[:middle], "tok", UP)))
    got.append((NZ // 2, middle, lax.ppermute(down[middle:], "tok", DOWN)))
    return got


def turned(x, cos, sin):
    return x * cos + pltpu.roll(x, HS // 2, 1) * sin


def norm_kv_kernel(x_ref, gain_ref, wk_ref, wv_ref, cos_ref, sin_ref, normed_ref, kv_ref):
    total = jnp.zeros((ROWS, 1), F32)
    for c in range(NTP):
        x = x_ref[c].astype(F32)
        total += jnp.sum(x * x, axis=1, keepdims=True)
    factor = lax.rsqrt(total / (NTP * COLS) + EPS)
    k = jnp.zeros((ROWS, HS), F32)
    v = jnp.zeros((ROWS, HS), F32)
    for c in range(NTP):
        normed = (x_ref[c].astype(F32) * factor * gain_ref[c : c + 1, :]).astype(BF16)
        normed_ref[c] = normed
        k += jnp.dot(normed, wk_ref[c * COLS : (c + 1) * COLS, :], preferred_element_type=F32)
        v += jnp.dot(normed, wv_ref[c * COLS : (c + 1) * COLS, :], preferred_element_type=F32)
    kv_ref[:ROWS, :] = turned(k, cos_ref[...], sin_ref[...]).astype(BF16)
    kv_ref[ROWS:, :] = v.astype(BF16)


def query_kernel(normed_ref, wq_ref, cos_ref, sin_ref, q_ref, weights, sems):
    def copy(c):
        part = pl.ds(c * COLS, COLS)
        return pltpu.make_async_copy(wq_ref.at[part], weights.at[part], sems.at[c])

    for c in range(NTP):
        copy(c).start()
    acc = jnp.zeros((ROWS, HEADS * HS), F32)
    for c in range(NTP):
        copy(c).wait()
        part = weights[c * COLS : (c + 1) * COLS, :]
        acc += jnp.dot(normed_ref[c], part, preferred_element_type=F32)
    for h in range(HEADS):
        q = turned(acc[:, h * HS : (h + 1) * HS], cos_ref[...], sin_ref[...])
        q_ref[:, h * ROWS : (h + 1) * ROWS] = q.T.astype(BF16)


def land(places, z, refs, held, sems):
    copies = []
    for i, ((far, row), ref) in enumerate(zip(places, refs)):
        at = lax.rem(z + NZ - far, NZ)
        copies.append(
            pltpu.make_async_copy(ref, held.at[at, pl.ds(row, ref.shape[0])], sems.at[i])
        )
    return copies


def attend_kernel(places, where_ref, starts_ref, q_mine_ref, q_other_ref, *rest):
    n = len(places)
    kv_refs, (mine_ref, other_ref, kv, sems) = rest[:n], rest[n:]
    z, y, k = where_ref[0], where_ref[1], where_ref[2]
    scale = math.log2(math.e) * HS**-0.5
    copies = land(places, z, kv_refs, kv, sems)
    for copy in copies:
        copy.start()
    for ref in (mine_ref, other_ref):
        ref[...] = jnp.zeros_like(ref)
        ref[HS : HS + 1, :] = jnp.full((1, HEADS * ROWS), NEG, F32)
    for copy in copies:
        copy.wait()

    for tile, (q_ref, acc_ref) in enumerate(((q_mine_ref, mine_ref), (q_other_ref, other_ref))):
        core = k if tile == 0 else 1 - k
        q_at = ((z * NY + y) * NC + core) * ROWS
        first, last = where_ref[3 + 2 * tile], where_ref[4 + 2 * tile]
        starts = starts_ref[tile : tile + 1, :]

        def block(plane, j, masked):
            k_at = ((plane * NY + lax.rem(y + j, NY)) * NC + k) * ROWS
            keys = kv[plane, 2 * j * ROWS : (2 * j + 1) * ROWS, :]
            values = kv[plane, (2 * j + 1) * ROWS : (2 * j + 2) * ROWS, :]
            if masked:
                key_pos = k_at + lax.broadcasted_iota(jnp.int32, (ROWS, ROWS), 0)
                query_pos = q_at + lax.broadcasted_iota(jnp.int32, (ROWS, ROWS), 1)
                kept = (key_pos <= query_pos) & (key_pos >= starts)
            ats = [slice(h * ROWS, (h + 1) * ROWS) for h in range(HEADS)]
            ss = [jnp.dot(keys, q_ref[:, at], preferred_element_type=F32) for at in ats]
            vt = values.T
            ws = []
            for at, s in zip(ats, ss):
                if masked:
                    s = jnp.where(kept, s, NEG)
                old = acc_ref[HS : HS + 1, at]
                top = jnp.maximum(old, jnp.max(s, axis=0, keepdims=True) * scale)
                w = jnp.exp2(s * scale - top)
                fade = jnp.exp2(old - top)
                acc_ref[HS : HS + 1, at] = top
                acc_ref[HS + 1 : HS + 2, at] = acc_ref[HS + 1 : HS + 2, at] * fade + jnp.sum(
                    w, axis=0, keepdims=True
                )
                ws.append((fade, w.astype(BF16)))
            for at, (fade, w) in zip(ats, ws):
                acc_ref[:HS, at] = acc_ref[:HS, at] * fade + jnp.dot(vt, w, preferred_element_type=F32)

        def wide(plane):
            ats = [slice(h * ROWS, (h + 1) * ROWS) for h in range(HEADS)]
            k0, k1 = kv[plane, :ROWS, :], kv[plane, 2 * ROWS : 3 * ROWS, :]
            ss = [
                (
                    jnp.dot(k0, q_ref[:, at], preferred_element_type=F32),
                    jnp.dot(k1, q_ref[:, at], preferred_element_type=F32),
                )
                for at in ats
            ]
            vt = jnp.concatenate([kv[plane, ROWS : 2 * ROWS, :], kv[plane, 3 * ROWS :, :]]).T
            ws = []
            for at, (s0, s1) in zip(ats, ss):
                old = acc_ref[HS : HS + 1, at]
                top = jnp.maximum(old, jnp.max(jnp.maximum(s0, s1), axis=0, keepdims=True) * scale)
                w0 = jnp.exp2(s0 * scale - top)
                w1 = jnp.exp2(s1 * scale - top)
                fade = jnp.exp2(old - top)
                acc_ref[HS : HS + 1, at] = top
                acc_ref[HS + 1 : HS + 2, at] = acc_ref[HS + 1 : HS + 2, at] * fade + jnp.sum(
                    w0 + w1, axis=0, keepdims=True
                )
                ws.append((fade, jnp.concatenate([w0.astype(BF16), w1.astype(BF16)])))
            for at, (fade, w) in zip(ats, ws):
                acc_ref[:HS, at] = acc_ref[:HS, at] * fade + jnp.dot(vt, w, preferred_element_type=F32)

        @pl.loop(0, NZ)
        def _(plane):
            low = plane * NY * NC * ROWS
            high = ((plane * NY + 1) * NC + k) * ROWS
            clear = (high < q_at) & (low >= last)

            @pl.when(clear)
            def _():
                wide(plane)

            for j in range(NY):
                k_at = ((plane * NY + lax.rem(y + j, NY)) * NC + k) * ROWS
                needed = (k_at <= q_at) & (k_at + ROWS > first) & jnp.logical_not(clear)
                whole = (k_at < q_at) & (k_at >= last)

                @pl.when(needed & whole)
                def _():
                    block(plane, j, False)

                @pl.when(needed & jnp.logical_not(whole))
                def _():
                    block(plane, j, True)


def project_kernel(mine_ref, came_ref, w_ref, out_ref, weights, att, sems):
    def copy(c):
        part = pl.ds(c * COLS, COLS)
        return pltpu.make_async_copy(w_ref.at[:, part], weights.at[c], sems.at[c])

    for c in range(NTP):
        copy(c).start()
    for h in range(HEADS):
        at = slice(h * ROWS, (h + 1) * ROWS)
        a, b = mine_ref[HS : HS + 1, at], came_ref[HS : HS + 1, at]
        top = jnp.maximum(a, b)
        fa, fb = jnp.exp2(a - top), jnp.exp2(b - top)
        weight_sum = mine_ref[HS + 1 : HS + 2, at] * fa + came_ref[HS + 1 : HS + 2, at] * fb
        blended = (mine_ref[:HS, at] * fa + came_ref[:HS, at] * fb) / weight_sum
        att[:, h * HS : (h + 1) * HS] = blended.T.astype(BF16)
    for c in range(NTP):
        copy(c).wait()
        out_ref[c] = jnp.dot(att[...], weights[c], preferred_element_type=F32).astype(BF16)


def gram_part(acc, rows, cols):
    acc[...] += jnp.dot(rows, cols, preferred_element_type=F32)


def add_sums(rows, row_sum, cols, col_sum):
    wide = rows.astype(F32)
    row_sum[...] += sum(wide[:, at : at + HS] for at in range(0, rows.shape[1], HS))
    col_sum[0:1, :] += jnp.sum(cols.astype(F32), axis=0, keepdims=True)


def gram_in_kernel(places, where_ref, rows_ref, *args):
    n = len(places)
    refs, (acc, row_sum, col_sum, rows, cols, sems) = args[:n], args[n:]
    z = where_ref[0]
    for far in range(NZ):
        here = lax.rem(2 * z + NZ - far, NTP)
        pltpu.make_async_copy(rows_ref.at[here], rows.at[far], sems.at[0, far]).start()
    for (far, row), ref in zip(places, refs):
        to = cols.at[far, pl.ds(row, ref.shape[0])]
        pltpu.make_async_copy(ref, to, sems.at[1, far]).start()
    for ref in (acc, row_sum, col_sum):
        ref[...] = jnp.zeros_like(ref)

    @pl.loop(0, NZ)
    def _(far):
        pltpu.make_async_copy(rows_ref.at[0], rows.at[far], sems.at[0, far]).wait()
        pltpu.make_async_copy(cols.at[far], cols.at[far], sems.at[1, far]).wait()
        gram_part(acc, rows[far], cols[far])
        add_sums(rows[far], row_sum, cols[far], col_sum)


def gram_kernel(places, *args):
    where_ref, rows_in_ref, rows_out_ref, cols_in_ref, ii, row_sum_in, col_sum_in = args[:7]
    args, n = args[7:], len(places)
    refs, (mine_ref, other_ref) = args[:n], args[n : n + 2]
    rows_in, rows_out, cols_in, cols_out, io, oi, oo, row_sum, col_sum, sems = args[n + 2 :]
    z, k = where_ref[0], where_ref[2]

    def copies(far):
        here = lax.rem(2 * z + NZ - far, NTP)
        return (
            pltpu.make_async_copy(rows_out_ref.at[here], rows_out.at[far], sems.at[0, far]),
            pltpu.make_async_copy(rows_in_ref.at[far], rows_in.at[far], sems.at[1, far]),
            pltpu.make_async_copy(cols_in_ref.at[far], cols_in.at[far], sems.at[2, far]),
        )

    def block_copies(far):
        for (at, row), ref in zip(places, refs):
            if at == far:
                to = cols_out.at[far, pl.ds(row, ref.shape[0])]
                pltpu.make_async_copy(ref, to, sems.at[3, far]).start()

    ahead = 4
    for far in range(ahead):
        for copy in copies(far):
            copy.start()
        block_copies(far)
    for ref in (io, oi, oo, row_sum, col_sum):
        ref[...] = jnp.zeros_like(ref)

    @pl.loop(0, NZ)
    def _(far):
        @pl.when(far + ahead < NZ)
        def _():
            for copy in copies(far + ahead):
                copy.start()

        for later in range(ahead, NZ):

            @pl.when(far + ahead == later)
            def _():
                block_copies(later)

        for copy in copies(far):
            copy.wait()
        pltpu.make_async_copy(cols_out.at[far], cols_out.at[far], sems.at[3, far]).wait()
        gram_part(io, rows_in[far], cols_out[far])
        gram_part(oi, rows_out[far], cols_in[far])
        gram_part(oo, rows_out[far], cols_out[far])
        add_sums(rows_out[far], row_sum, cols_out[far], col_sum)

    for core, ref in ((k, mine_ref), (1 - k, other_ref)):
        rows = pl.ds(pl.multiple_of(core * HS, HS), HS)
        for at, (left, right, sums) in ((0, (ii, io, row_sum_in)), (HS, (oi, oo, row_sum))):
            ref[at : at + HS, :COLS] = left[rows, :]
            ref[at : at + HS, COLS : 2 * COLS] = right[rows, :]
            ref[at : at + HS, 2 * COLS :] = sums[rows, :]
        ref[2 * HS :, :COLS] = col_sum_in[...]
        ref[2 * HS :, COLS : 2 * COLS] = col_sum[...]
        ref[2 * HS :, 2 * COLS :] = jnp.zeros((8, HS), F32)


def finish_kernel(tokens, mine_ref, came_ref, out_ref):
    col_mean = (mine_ref[2 * HS :, :] + came_ref[2 * HS :, :])[0:1, : 2 * COLS] / tokens
    row_sums = mine_ref[: 2 * HS, 2 * COLS :] + came_ref[: 2 * HS, 2 * COLS :]
    row_mean = jnp.sum(row_sums, axis=1, keepdims=True) / tokens
    for a in range(2):
        for b in range(2):
            rows, cols = slice(a * HS, (a + 1) * HS), slice(b * COLS, (b + 1) * COLS)
            gram = mine_ref[rows, cols] + came_ref[rows, cols]
            out_ref[a, :, b, :] = gram / tokens - row_mean[rows, :] * col_mean[:, cols]


def on_device(hidden_in, norm_gain, w_query, w_key, w_value, w_out, doc_ids):
    tok_index = lax.axis_index("tok")
    z, y, k = tok_index // (NY * NC), (tok_index // NC) % NY, tok_index % NC
    tokens = ROWS * NZ * NY * NC

    first_row = tok_index * ROWS
    other_row = (tok_index + 1 - 2 * k) * ROWS
    doc_start = jnp.stack([jnp.sum((doc_ids < d).astype(jnp.int32)) for d in range(4)])

    def starts_of(row):
        docs = lax.dynamic_slice_in_dim(doc_ids, row, ROWS, 0)
        return sum(jnp.where(docs == d, doc_start[d], 0) for d in range(4))

    starts = jnp.stack([starts_of(first_row), starts_of(other_row)])
    place = jnp.stack([z, y, k]).astype(jnp.int32)
    ends = jnp.stack([starts[0, 0], starts[0, -1], starts[1, 0], starts[1, -1]])
    where = jnp.concatenate([place, ends]).astype(jnp.int32)
    inv_freq = ROPE_BASE ** (-(jnp.arange(HS // 2, dtype=F32) * 2.0) / HS)
    positions = first_row + jnp.arange(ROWS, dtype=jnp.int32)
    angles = positions.astype(F32)[:, None] * inv_freq[None, :]
    cosine, sine = jnp.cos(angles), jnp.sin(angles)
    cos = jnp.concatenate([cosine, cosine], axis=1)
    sin = jnp.concatenate([-sine, sine], axis=1)

    def rows_in_plane(x):
        here = lax.dynamic_slice_in_dim(x, y * HALF, HALF, 1).T
        there = lax.dynamic_slice_in_dim(x, (1 - y) * HALF, HALF, 1).T
        here = lax.ppermute(here, BOTH, IN_PLANE)
        there = lax.ppermute(there, BOTH, IN_PLANE_OTHER_Y)
        return jnp.concatenate([here, there], axis=1)

    full_in = gather_tp(copies_for_tp(hidden_in))
    in_blocks = ring(hidden_in)
    rows_in = rows_in_plane(hidden_in)
    early = [b[2] for b in in_blocks]
    full_in = after(full_in, cos, sin, where, starts, rows_in, *early)
    normed, kv = pl.pallas_call(
        norm_kv_kernel,
        out_shape=(
            jax.ShapeDtypeStruct((NTP, ROWS, COLS), BF16),
            jax.ShapeDtypeStruct((2 * ROWS, HS), BF16),
        ),
        in_specs=[VMEM] * 6,
        out_specs=(VMEM, VMEM),
        compiler_params=params(14),
        cost_estimate=cost(1 << 30, 6 << 20),
        name="norm_kv",
    )(full_in, norm_gain.reshape(NTP, COLS), w_key, w_value, cos, sin)
    kv_pair = jnp.concatenate([kv, lax.ppermute(kv, "tok", OTHER_Y)])

    q = pl.pallas_call(
        query_kernel,
        out_shape=jax.ShapeDtypeStruct((HS, HEADS * ROWS), BF16),
        in_specs=[VMEM, ANY, VMEM, VMEM],
        out_specs=VMEM,
        scratch_shapes=[
            pltpu.VMEM((NTP * COLS, HEADS * HS), BF16),
            pltpu.SemaphoreType.DMA((NTP,)),
        ],
        compiler_params=params(60),
        cost_estimate=cost(1 << 30, 6 << 20),
        name="queries",
    )(normed, w_query, cos, sin)
    in_other = lax.ppermute(after(hidden_in, kv), "tok", OTHER_Y)
    moved = lax.ppermute(rows_in, BOTH, TO_PLANE)
    kv_blocks = ring(kv_pair, {3: (moved, q)})
    rows_in = gather_tp(copies_for_tp(after(moved, kv_blocks[5][2], kv_blocks[6][2])))
    other_blocks = ring(after(in_other, kv_blocks[5][2]))
    q_other = lax.ppermute(q, "tok", OTHER_CORE)

    half = jax.ShapeDtypeStruct((HS + 8, HEADS * ROWS), F32)
    mine, other = pl.pallas_call(
        functools.partial(attend_kernel, [b[:2] for b in kv_blocks]),
        out_shape=(half, half),
        in_specs=[SMEM, VMEM, VMEM, VMEM] + [ANY] * len(kv_blocks),
        out_specs=(VMEM, VMEM),
        scratch_shapes=[
            pltpu.VMEM((NZ, 2 * NY * ROWS, HS), BF16),
            pltpu.SemaphoreType.DMA((len(kv_blocks),)),
        ],
        compiler_params=params(60),
        cost_estimate=cost(16 << 30, 6 << 20),
        name="attend",
    )(after(where, in_other), starts, q, q_other, *[b[2] for b in kv_blocks])
    came = lax.ppermute(other, "tok", OTHER_CORE)

    partial_out = pl.pallas_call(
        project_kernel,
        out_shape=jax.ShapeDtypeStruct((NTP, ROWS, COLS), BF16),
        in_specs=[VMEM, VMEM, ANY],
        out_specs=VMEM,
        scratch_shapes=[
            pltpu.VMEM((NTP, HEADS * HS, COLS), BF16),
            pltpu.VMEM((ROWS, HEADS * HS), BF16),
            pltpu.SemaphoreType.DMA((NTP,)),
        ],
        compiler_params=params(60),
        cost_estimate=cost(1 << 30, 8 << 20),
        name="project",
    )(mine, came, w_out)
    shares = lax.all_to_all(partial_out, "tp", split_axis=0, concat_axis=0, tiled=True)

    shares = after(shares, rows_in, *[b[2] for b in other_blocks])
    hidden_out = (
        hidden_in.astype(F32) + jnp.sum(shares.astype(F32), axis=0)
    ).astype(BF16)

    rows_out = rows_in_plane(hidden_out)
    out_pair = jnp.concatenate([hidden_out, lax.ppermute(hidden_out, "tok", OTHER_Y)])
    moved = lax.ppermute(rows_out, BOTH, TO_PLANE)
    in_blocks += [(f, ROWS + r, b) for f, r, b in other_blocks]
    part = jax.ShapeDtypeStruct((HALF, COLS), F32)
    ii, row_sum_in, col_sum_in, rows_in, cols_in = pl.pallas_call(
        functools.partial(gram_in_kernel, [b[:2] for b in in_blocks]),
        out_shape=(
            part,
            jax.ShapeDtypeStruct((HALF, HS), F32),
            jax.ShapeDtypeStruct((8, COLS), F32),
            jax.ShapeDtypeStruct((NZ, HALF, NY * ROWS), BF16),
            jax.ShapeDtypeStruct((NZ, NY * ROWS, COLS), BF16),
        ),
        in_specs=[SMEM] + [ANY] * (1 + len(in_blocks)),
        out_specs=(VMEM,) * 5,
        scratch_shapes=[pltpu.SemaphoreType.DMA((2, NZ))],
        compiler_params=params(60),
        cost_estimate=cost(1 << 30, 12 << 20),
        name="gram_in",
    )(where, rows_in, *[b[2] for b in in_blocks])
    out_blocks = ring(after(out_pair, rows_out), {2: (moved,), 3: (ii,)})
    rows_out = gather_tp(copies_for_tp(moved))
    acc = pltpu.VMEM((HALF, COLS), F32)
    half = jax.ShapeDtypeStruct((2 * HS + 8, 2 * COLS + HS), F32)
    mine, other = pl.pallas_call(
        functools.partial(gram_kernel, [b[:2] for b in out_blocks]),
        out_shape=(half, half),
        in_specs=[SMEM] + [ANY] * 3 + [VMEM] * 3 + [ANY] * len(out_blocks),
        out_specs=(VMEM, VMEM),
        scratch_shapes=[
            pltpu.VMEM((NZ, HALF, NY * ROWS), BF16),
            pltpu.VMEM((NZ, HALF, NY * ROWS), BF16),
            pltpu.VMEM((NZ, NY * ROWS, COLS), BF16),
            pltpu.VMEM((NZ, NY * ROWS, COLS), BF16),
            acc,
            acc,
            acc,
            pltpu.VMEM((HALF, HS), F32),
            pltpu.VMEM((8, COLS), F32),
            pltpu.SemaphoreType.DMA((4, NZ)),
        ],
        compiler_params=params(60),
        cost_estimate=cost(6 << 30, 14 << 20),
        name="gram",
    )(
        where,
        rows_in,
        rows_out,
        cols_in,
        ii,
        row_sum_in,
        col_sum_in,
        *[b[2] for b in out_blocks],
    )
    joint_cov = pl.pallas_call(
        functools.partial(finish_kernel, tokens),
        out_shape=jax.ShapeDtypeStruct((2, HS, 2, COLS), F32),
        in_specs=[VMEM, VMEM],
        out_specs=VMEM,
        compiler_params=params(14),
        cost_estimate=cost(1 << 22, 3 << 20),
        name="finish",
    )(mine, lax.ppermute(other, "tok", OTHER_CORE))
    return hidden_out, joint_cov


def solution(mesh):
    return jax.shard_map(
        on_device,
        mesh=mesh,
        in_specs=(
            P("tok", "tp"),
            P(),
            P(None, "tp"),
            P(None, "tp"),
            P(None, "tp"),
            P("tp", None),
            P(),
        ),
        out_specs=(P("tok", "tp"), P(None, "tok", None, "tp")),
        check_vma=False,
    )
```
